512 devices in a mesh: blk: 16 (over z_lo, y), grp: 32 (over x, z_hi, core).
Axes of the slice: x: 4, y: 8, z: 8 (z_hi: 4, z_lo: 2; z = z_hi * 2 + z_lo), core: 2. Of those that a mesh axis runs over, the one named last changes fastest.
Arguments:
- image_cand: bfloat16 [131072, 1152], P(('blk', 'grp')), may hold values from -6 to 6
- text_cand: bfloat16 [131072, 1152], P(('blk', 'grp')), may hold values from -0.1796875 to 0.1796875
- selection: int32 [65536], P(('blk', 'grp')), may hold values from 0 to 255, as said below
- head_weight: bfloat16 [1152, 1152], P('grp'), may hold values from -0.1875 to 0.1875
- logit_temp: float32 [1], replicated, may hold values from 4 to 12
- logit_offset: float32 [1], replicated, may hold values from -5 to -2
- loss_scale: float32 [1], replicated, may hold values from 65536 to 262144
Outputs:
- head_grad: float32 [1152, 1152], P('grp')
- text_grad: float32 [131072, 1152], P(('blk', 'grp'))
The draws below stay inside these ranges and needn't reach their ends.
Inputs may be any that keep to these rules, and one draw needn't show every extreme that they name: `selection`: within one device's 128 entries the indices are distinct.
All inputs are finite; a program needn't handle non-finite values.
Results may differ from the reference program's by a relative error of at most 0.022.
Values may be sent and summed in bfloat16 or wider, within the bound.
No kernel may reach another device: no remote copies, remote signals or barrier semaphores. Data moves between devices by JAX's collectives and lax.ppermute only.
A program may use at most 64 MiB of HBM per device.

```python
import math
import jax
import jax.numpy as jnp
from jax import lax

D = 1152
E = 1152
PAIRS_DEV = 128
RATIO = 2
TOTAL = 65536
CANDS = 131072
N_BLK = 16
N_GRP = 32


def draw_selection(key, part):
    key = jax.random.fold_in(key, 5)
    blocks = TOTAL // PAIRS_DEV
    keys = jax.random.split(key, blocks)
    chosen = jax.vmap(lambda seed_key: jax.random.permutation(seed_key, RATIO * PAIRS_DEV))(keys)
    return chosen[:, :PAIRS_DEV].reshape(-1).astype(jnp.int32)


def levels(stream_key, shape, shards, low, high):
    def one(dim, shards_of):
        heights = jax.random.uniform(jax.random.fold_in(jax.random.fold_in(stream_key, 6), dim), (shards_of,), jnp.float32, low / len(shards), high / len(shards))
        return jnp.repeat(jnp.exp(heights), shape[dim] // shards_of).reshape((-1,) + (1,) * (len(shape) - dim - 1))

    gain = one(*shards[0])
    for cut in shards[1:]:
        gain = gain * one(*cut)
    return gain


def bell_draw(rng, extent, scale, bound, shards=(), kind=jnp.bfloat16):
    entries = jax.random.normal(rng, extent, jnp.float32) * scale
    if len(shards) > 0:
        entries = levels(rng, extent, shards, -0.22, 0.18) * entries
    return jnp.clip(entries, min=-bound, max=bound).astype(kind)


def setup_inputs(seed: int = 0) -> dict:
    key_of = jax.random.split(jax.random.key(seed), 8)
    image_cand = bell_draw(key_of[0], (CANDS, D), 1.0, 6.0, ((0, 512),))
    text_cand = bell_draw(key_of[1], (CANDS, E), 0.03, 0.1796875, ((0, 512),))
    selection = draw_selection(jax.random.fold_in(key_of[7], 71), 0)
    head_weight = bell_draw(key_of[3], (D, E), D ** -0.5, 0.1875, ((0, 32),))
    logit_temp = jnp.clip(jax.random.uniform(key_of[4], (1,), jnp.float32, 4.0, 12.0), 4.0, 12.0)
    logit_offset = jnp.clip(jax.random.uniform(key_of[5], (1,), jnp.float32, -5.0, -2.0), -5.0, -2.0)
    loss_scale = jnp.clip(jnp.exp(jax.random.uniform(key_of[6], (1,), jnp.float32, math.log(65536.0), math.log(262144.0))), 65536.0, 262144.0)
    return dict(image_cand=image_cand, text_cand=text_cand, selection=selection, head_weight=head_weight, logit_temp=logit_temp, logit_offset=logit_offset, loss_scale=loss_scale)


EPS = 1e-06

def by_member(values, width):
    shaped = values.reshape(N_BLK, N_GRP, PAIRS_DEV, width)
    return jnp.transpose(shaped, (1, 0, 2, 3)).reshape(N_GRP, N_BLK * PAIRS_DEV, width)

def from_member(values, width):
    shaped = values.reshape(N_GRP, N_BLK, PAIRS_DEV, width)
    return jnp.transpose(shaped, (1, 0, 2, 3)).reshape(N_GRP * N_BLK * PAIRS_DEV, width)

def reference(image_cand, text_cand, selection, head_weight, logit_temp, logit_offset, loss_scale):
    total_pairs = selection.shape[0]
    width = head_weight.shape[1]
    depth = head_weight.shape[0]
    pair_ids = jnp.arange(total_pairs, dtype=jnp.int32)
    row_index = (pair_ids // PAIRS_DEV * (RATIO * PAIRS_DEV) + selection).astype(jnp.int32)
    picked = image_cand[row_index]
    texts = text_cand[row_index].astype(jnp.float32)
    projected = jnp.dot(picked, head_weight, preferred_element_type=jnp.float32)
    img_norm = jnp.sqrt(lax.optimization_barrier(jnp.sum(projected * projected, axis=1)) + EPS)
    image_unit = (projected / img_norm[:, None]).astype(jnp.bfloat16)
    txt_norm = jnp.sqrt(lax.optimization_barrier(jnp.sum(texts * texts, axis=1)) + EPS)
    text_unit = (texts / txt_norm[:, None]).astype(jnp.bfloat16)
    temper = logit_temp[0]
    offset = logit_offset[0]
    factor = loss_scale[0] / total_pairs
    sub_ids = jnp.arange(N_BLK * PAIRS_DEV, dtype=jnp.int32)
    label_sign = jnp.where(sub_ids[:, None] == sub_ids[None, :], 1.0, -1.0).astype(jnp.float32)

    def member_step(carry, operands):
        image_blk, text_blk = operands
        inner = lax.dot_general(image_blk, text_blk, (((1,), (1,)), ((), ())), preferred_element_type=jnp.float32)
        logits = temper * inner + offset
        grad_tile = (-factor * label_sign * jax.nn.sigmoid(-label_sign * logits)).astype(jnp.bfloat16)
        image_back = temper * jnp.dot(grad_tile, text_blk, preferred_element_type=jnp.float32)
        text_back = temper * lax.dot_general(grad_tile, image_blk, (((0,), (0,)), ((), ())), preferred_element_type=jnp.float32)
        return (carry, (image_back, text_back))
    start_carry = jnp.zeros((), jnp.float32)
    unused, (image_member, text_member) = lax.scan(member_step, start_carry, (by_member(image_unit, width), by_member(text_unit, width)))
    image_back = from_member(image_member, width)
    text_back = from_member(text_member, width)
    unit_float = image_unit.astype(jnp.float32)
    radial = lax.optimization_barrier(jnp.sum(unit_float * image_back, axis=1, keepdims=True))
    proj_back = (image_back - unit_float * radial) / img_norm[:, None]

    def head_step(total, operands):
        picked_dev, back_dev = operands
        term = lax.dot_general(picked_dev.astype(jnp.float32), back_dev, (((0,), (0,)), ((), ())), precision=lax.Precision.HIGHEST, preferred_element_type=jnp.float32)
        rounded = lax.optimization_barrier(term.astype(jnp.bfloat16))
        return (total + rounded.astype(jnp.float32), None)
    head_grad, unused_two = lax.scan(head_step, jnp.zeros((depth, width), jnp.float32), (picked.reshape(-1, PAIRS_DEV, depth), proj_back.reshape(-1, PAIRS_DEV, width)))
    text_float = text_unit.astype(jnp.float32)
    text_radial = lax.optimization_barrier(jnp.sum(text_float * text_back, axis=1, keepdims=True))
    text_rows = (text_back - text_float * text_radial) / txt_norm[:, None]
    text_grad = jnp.zeros((text_cand.shape[0], width), jnp.float32).at[row_index].set(text_rows)
    return (head_grad, text_grad)
```

```python
import jax
import jax.numpy as jnp
from jax import lax
from jax.sharding import Mesh, PartitionSpec as P

EPS = 1e-06
ALL = ("zl", "y", "x", "zh", "c")
WIDE = 640


def ring(axis, steps):
    count = lax.axis_size(axis)
    return [(source, (source + steps) % count) for source in range(count)]


def hop(value, axis, steps):
    return lax.ppermute(value, axis, ring(axis, steps))


def gather_weight(head_weight):
    core = lax.axis_index("c")
    place = lax.axis_index("x")
    rows = lax.all_gather(head_weight, "c", axis=0, tiled=True)
    width = rows.shape[1]
    part = lax.dynamic_slice(rows, (0, core * (width - WIDE)), (rows.shape[0], WIDE))
    slab = lax.all_gather(part, "zh", axis=0, tiled=True)
    before = hop(slab, "x", 1)
    after = hop(slab, "x", -1)
    half = slab.shape[0] // 2
    far_low = hop(after[:half], "x", -1)
    far_high = hop(before[half:], "x", 1)
    far = jnp.concatenate([far_low, far_high], axis=0)
    count = lax.axis_size("x")
    held = jnp.zeros((count,) + slab.shape, slab.dtype)
    for steps, block in ((0, slab), (-1, before), (1, after), (2, far)):
        spot = lax.rem(place + steps + count, count)
        held = lax.dynamic_update_slice(held, block[None], (spot, 0, 0))
    mine = held.reshape(count * slab.shape[0], WIDE)
    other = hop(mine, "c", 1)
    low = jnp.where(core == 0, mine, other)
    high = jnp.where(core == 0, other, mine)
    return low, high


def shards(image_cand, text_cand, selection, head_weight, logit_temp, logit_offset, loss_scale):
    pairs = selection.shape[0]
    depth = image_cand.shape[1]
    width = head_weight.shape[1]
    n_y, n_x, n_zh = lax.axis_size("y"), lax.axis_size("x"), lax.axis_size("zh")
    my_zl, my_y, core = lax.axis_index("zl"), lax.axis_index("y"), lax.axis_index("c")
    total = pairs * lax.axis_size(ALL)

    picked = image_cand.at[selection].get(mode="promise_in_bounds")
    images = lax.all_gather(picked, "y", axis=0, tiled=True)
    texts = text_cand.at[selection].get(mode="promise_in_bounds").astype(jnp.float32)
    txt_norm = jnp.sqrt(jnp.sum(texts * texts, axis=1, keepdims=True) + EPS)
    text_unit = (texts / txt_norm).astype(jnp.bfloat16)
    text_pair = lax.all_gather(text_unit, "zl", axis=0, tiled=True)

    low, high = gather_weight(head_weight)
    proj_low = jnp.dot(images, low, preferred_element_type=jnp.float32)
    proj_high = jnp.dot(images, high[:, 2 * WIDE - width:], preferred_element_type=jnp.float32)
    projected = jnp.concatenate([proj_low, proj_high], axis=1)
    img_norm = jnp.sqrt(jnp.sum(projected * projected, axis=1, keepdims=True) + EPS)
    image_unit = (projected / img_norm).astype(jnp.bfloat16)

    temper, offset = logit_temp[0], logit_offset[0]
    factor = loss_scale[0] / total
    row_id = jnp.arange(n_y * pairs, dtype=jnp.int32)[:, None]
    col_id = jnp.arange(2 * pairs, dtype=jnp.int32)[None, :]
    same = (row_id - my_y * pairs == col_id - my_zl * pairs) & (row_id // pairs == my_y)
    label_sign = jnp.where(same, 1.0, -1.0).astype(jnp.float32)
    inner = lax.dot_general(image_unit, text_pair, (((1,), (1,)), ((), ())), preferred_element_type=jnp.float32)
    logits = temper * inner + offset
    grad_tile = (-factor * label_sign * jax.nn.sigmoid(-label_sign * logits)).astype(jnp.bfloat16)

    image_back = temper * jnp.dot(grad_tile, text_pair, preferred_element_type=jnp.float32)
    unit_float = image_unit.astype(jnp.float32)
    radial = jnp.sum(unit_float * image_back, axis=1, keepdims=True)
    proj_back = ((image_back - unit_float * radial) / img_norm).astype(jnp.bfloat16)

    def head_half(values):
        return lax.dot_general(images, values, (((0,), (0,)), ((), ())), preferred_element_type=jnp.float32)

    mid = width // 2
    halves = [proj_back[:, :mid], proj_back[:, mid:]]
    mine_cols = jnp.where(core == 0, halves[0], halves[1])
    other_cols = jnp.where(core == 0, halves[1], halves[0])
    send = head_half(other_cols).astype(jnp.bfloat16)
    got = hop(send, "c", 1)
    head = head_half(mine_cols) + got.astype(jnp.float32)

    tile_t = lax.dot_general(grad_tile, image_unit, (((0,), (0,)), ((), ())), preferred_element_type=jnp.float32)
    text_mine = lax.dynamic_slice(tile_t, (my_zl * pairs, 0), (pairs, width))
    text_other = lax.dynamic_slice(tile_t, ((1 - my_zl) * pairs, 0), (pairs, width)).astype(jnp.bfloat16)
    text_got = hop(text_other, "zl", 1)

    def spread(values, axis):
        count = lax.axis_size(axis)
        parts = values.astype(jnp.bfloat16).reshape(count, values.shape[0] // count, values.shape[1])
        came = lax.all_to_all(parts, axis, 0, 0)
        return jnp.sum(came.astype(jnp.float32), axis=0)

    head = spread(head, "x")
    head = spread(head, "zh")
    both = lax.all_gather(head.astype(jnp.bfloat16), "c", axis=0)
    half_rows = head.shape[0] // 2
    both = lax.dynamic_slice(both, (0, core * half_rows, 0), (2, half_rows, mid))
    head = jnp.concatenate([both[0], both[1]], axis=1)
    head = jnp.sum(lax.all_gather(head, "zl", axis=0).astype(jnp.float32), axis=0)
    head_grad = jnp.sum(lax.all_gather(head.astype(jnp.bfloat16), "y", axis=0).astype(jnp.float32), axis=0)

    text_back = temper * (text_mine + text_got.astype(jnp.float32))
    text_float = text_unit.astype(jnp.float32)
    text_radial = jnp.sum(text_float * text_back, axis=1, keepdims=True)
    text_rows = (text_back - text_float * text_radial) / txt_norm
    text_grad = jnp.zeros((text_cand.shape[0], width), jnp.float32).at[selection].set(
        text_rows, mode="promise_in_bounds", unique_indices=True)
    return head_grad, text_grad


def solution(mesh):
    devices = mesh.devices
    fine = Mesh(devices.reshape(2, devices.shape[0] // 2, 4, devices.shape[1] // 8, 2), ALL)
    return jax.shard_map(
        shards,
        mesh=fine,
        in_specs=(P(ALL, None), P(ALL, None), P(ALL), P(("x", "zh", "c"), None), P(), P(), P()),
        out_specs=(P(("x", "zh", "c"), None), P(ALL, None)),
        check_vma=False,
    )
```

```python
import functools

import jax
import jax.numpy as jnp
from jax import lax
from jax.experimental import pallas as pl
from jax.experimental.pallas import tpu as pltpu
from jax.sharding import Mesh, PartitionSpec as P

EPS = 1e-06
ALL = ("zl", "y", "x", "zh", "c")
WIDE = 640
CHUNK = 256
VMEM = pl.BlockSpec(memory_space=pltpu.VMEM)
SMEM = pl.BlockSpec(memory_space=pltpu.SMEM)
PARAMS = pltpu.CompilerParams(vmem_limit_bytes=48 * 1024 * 1024)


def hop(value, axis, steps):
    count = lax.axis_size(axis)
    return lax.ppermute(value, axis, [(s, (s + steps) % count) for s in range(count)])


def nn(a, b):
    return jnp.dot(a, b, preferred_element_type=jnp.float32)


def nt(a, b):
    return lax.dot_general(a, b, (((1,), (1,)), ((), ())), preferred_element_type=jnp.float32)


def project_kernel(core_ref, x_ref, *refs):
    pieces, (unit_ref, norm_ref, proj_ref) = refs[:10], refs[10:]
    width = unit_ref.shape[1]
    half = pieces[3].shape[0]
    sums = []
    for own, before, after, far_low, far_high in (pieces[:5], pieces[5:]):
        total = nn(x_ref[0], own[...]) + nn(x_ref[1], before[...]) + nn(x_ref[2], after[...])
        total += nn(x_ref[3, :, :half], far_low[...]) + nn(x_ref[3, :, half:], far_high[...])
        sums.append(total)
    mine, other = sums
    first = core_ref[0] == 0
    proj_ref[:, :WIDE] = jnp.where(first, mine, other)
    proj_ref[:, WIDE:] = jnp.where(first, other, mine)[:, 2 * WIDE - width:]
    proj = proj_ref[...]
    norm = jnp.sqrt(jnp.sum(proj * proj, axis=1, keepdims=True) + EPS)
    unit_ref[...] = (proj / norm).astype(jnp.bfloat16)
    norm_ref[...] = norm


def tile_kernel(scal_ref, spot_ref, unit_ref, norm_ref, text_ref, cols_ref, send_ref, back_ref, grad_ref, total_ref):
    temper, offset, factor = scal_ref[0], scal_ref[1], scal_ref[2]
    rows = unit_ref.shape[0]
    unit = unit_ref[...]
    pair = rows // 2
    row_id = lax.broadcasted_iota(jnp.int32, (rows, CHUNK), 0) - spot_ref[0]
    col_id = lax.broadcasted_iota(jnp.int32, (rows, CHUNK), 1) - spot_ref[1]
    inside = (row_id >= 0) & (row_id < pair)
    for k in range(text_ref.shape[0] // CHUNK):
        text = text_ref[k * CHUNK:(k + 1) * CHUNK, :]
        logits = temper * nt(unit, text) + offset
        same = inside & (col_id + k * CHUNK == row_id)
        sign = jnp.where(same, 1.0, -1.0)
        grad = (-factor * sign / (1.0 + jnp.exp(sign * logits))).astype(jnp.bfloat16)
        grad_ref[:, k * CHUNK:(k + 1) * CHUNK] = grad
        part = nn(grad, text)
        if k == 0:
            total_ref[...] = part
        else:
            total_ref[...] += part
    image_back = temper * total_ref[...]
    unit_float = unit.astype(jnp.float32)
    radial = jnp.sum(unit_float * image_back, axis=1, keepdims=True)
    back = ((image_back - unit_float * radial) / norm_ref[...]).astype(jnp.bfloat16)
    back_ref[...] = back
    send_ref[...] = nn(cols_ref[...], back).astype(jnp.bfloat16)


def gather_weight(head_weight, after_this):
    core = lax.axis_index("c")
    rows = lax.all_gather(head_weight, "c", axis=0, tiled=True)
    width = rows.shape[1]
    part = lax.dynamic_slice(rows, (0, core * (width - WIDE)), (rows.shape[0], WIDE))
    slab = lax.all_gather(part, "zh", axis=0, tiled=True)
    slab, after_this = lax.optimization_barrier((slab, after_this))
    before = hop(slab, "x", 1)
    after = hop(slab, "x", -1)
    half = slab.shape[0] // 2
    far_low = hop(after[:half], "x", -1)
    far_high = hop(before[half:], "x", 1)
    mine = (slab, before, after, far_low, far_high)
    other = tuple(hop(piece, "c", 1) for piece in mine)
    return mine + other, after_this


def shards(image_cand, text_cand, selection, head_weight, logit_temp, logit_offset, loss_scale):
    pairs = selection.shape[0]
    depth = image_cand.shape[1]
    width = head_weight.shape[1]
    n_y, n_x, n_z = lax.axis_size("y"), lax.axis_size("x"), lax.axis_size(("zh", "zl"))
    my_zl, my_y, my_x, core = (lax.axis_index(a) for a in ("zl", "y", "x", "c"))
    total = pairs * lax.axis_size(ALL)
    own_rows = head_weight.shape[0]

    texts = text_cand.at[selection].get(mode="promise_in_bounds").astype(jnp.float32)
    txt_norm = jnp.sqrt(jnp.sum(texts * texts, axis=1, keepdims=True) + EPS)
    text_unit = (texts / txt_norm).astype(jnp.bfloat16)
    text_all = lax.all_gather(text_unit, "y", axis=0, tiled=True)

    picked = image_cand.at[selection].get(mode="promise_in_bounds")
    pieces, picked = gather_weight(head_weight, picked)
    there = hop(picked, "zl", 1)
    images = jnp.concatenate([jnp.where(my_zl == 0, picked, there), jnp.where(my_zl == 0, there, picked)], axis=0)

    rows = images.shape[0]
    by_x = images.reshape(rows, n_x, depth // n_x).transpose(1, 0, 2)
    by_x = jnp.stack([by_x[lax.rem(my_x + s + n_x, n_x)] for s in (0, -1, 1, 2)])
    by_core = images.T.reshape(depth // (2 * own_rows), 2, own_rows, rows).transpose(1, 0, 2, 3)
    by_core = by_core.reshape(2, depth // 2, rows)
    cols_mine, cols_other = by_core[core], by_core[1 - core]

    image_unit, img_norm = pl.pallas_call(
        project_kernel,
        out_shape=(jax.ShapeDtypeStruct((rows, width), jnp.bfloat16), jax.ShapeDtypeStruct((rows, 1), jnp.float32)),
        in_specs=[SMEM] + [VMEM] * 11,
        out_specs=(VMEM, VMEM),
        scratch_shapes=[pltpu.VMEM((rows, width), jnp.float32)],
        compiler_params=PARAMS,
        cost_estimate=pl.CostEstimate(flops=2 * rows * depth * width, bytes_accessed=4_000_000, transcendentals=0),
    )(core[None], by_x, *pieces)

    temper = logit_temp[0]
    factor = loss_scale[0] / total
    scalars = jnp.stack([temper, logit_offset[0], factor])
    spot = jnp.stack([my_zl * pairs, my_y * pairs])
    send, proj_back, grad_tile = pl.pallas_call(
        tile_kernel,
        out_shape=(
            jax.ShapeDtypeStruct((depth // 2, width), jnp.bfloat16),
            jax.ShapeDtypeStruct((rows, width), jnp.bfloat16),
            jax.ShapeDtypeStruct((rows, n_y * pairs), jnp.bfloat16),
        ),
        in_specs=[SMEM, SMEM] + [VMEM] * 4,
        out_specs=(VMEM, VMEM, VMEM),
        scratch_shapes=[pltpu.VMEM((rows, width), jnp.float32)],
        compiler_params=PARAMS,
        cost_estimate=pl.CostEstimate(flops=5 * rows * n_y * pairs * width, bytes_accessed=4_000_000, transcendentals=0),
    )(scalars, spot, image_unit, img_norm, text_all, cols_other)

    got = hop(send, "c", 1)
    head = nn(cols_mine, proj_back) + got.astype(jnp.float32)

    text_part = lax.dot_general(grad_tile, image_unit, (((0,), (0,)), ((), ())), preferred_element_type=jnp.float32)
    text_part = (temper * text_part).astype(jnp.bfloat16).reshape(n_y, pairs, width)
    text_back = lax.psum_scatter(text_part, "y", scatter_dimension=0).astype(jnp.float32)

    def spread(values, axis):
        count = lax.axis_size(axis)
        parts = values.astype(jnp.bfloat16).reshape(count, values.shape[0] // count, values.shape[1])
        return jnp.sum(lax.all_to_all(parts, axis, 0, 0).astype(jnp.float32), axis=0)

    head = spread(head, "x")
    head = spread(head, ("zh", "zl"))
    copies = jnp.broadcast_to(head.astype(jnp.bfloat16)[None], (n_y,) + head.shape)
    head = jnp.sum(lax.all_to_all(copies, "y", 0, 0).astype(jnp.float32), axis=0)
    head_grad = lax.all_gather(head, "zl", axis=0, tiled=True)

    text_float = text_unit.astype(jnp.float32)
    text_radial = jnp.sum(text_float * text_back, axis=1, keepdims=True)
    text_rows = (text_back - text_float * text_radial) / txt_norm
    text_grad = jnp.zeros((text_cand.shape[0], width), jnp.float32).at[selection].set(
        text_rows, mode="promise_in_bounds", unique_indices=True)
    return head_grad, text_grad


def solution(mesh):
    devices = mesh.devices
    fine = Mesh(devices.reshape(2, devices.shape[0] // 2, 4, devices.shape[1] // 8, 2), ALL)
    return jax.shard_map(
        shards,
        mesh=fine,
        in_specs=(P(ALL, None), P(ALL, None), P(ALL), P(("x", "zh", "c"), None), P(), P(), P()),
        out_specs=(P(("x", "zh", "c"), None), P(ALL, None)),
        check_vma=False,
    )
```

```python
import jax
import jax.numpy as jnp
from jax import lax
from jax.experimental import pallas as pl
from jax.experimental.pallas import tpu as pltpu
from jax.sharding import Mesh, PartitionSpec as P

EPS = 1e-06
ALL = ("zl", "y", "x", "zh", "c")
WIDE = 640
CHUNK = 256
VMEM = pl.BlockSpec(memory_space=pltpu.VMEM)
SMEM = pl.BlockSpec(memory_space=pltpu.SMEM)
ANY = pl.BlockSpec(memory_space=pl.ANY)
PARAMS = pltpu.CompilerParams(vmem_limit_bytes=40 * 1024 * 1024)
F32, BF16 = jnp.float32, jnp.bfloat16


def hop(value, axis, steps):
    count = lax.axis_size(axis)
    return lax.ppermute(value, axis, [(s, (s + steps) % count) for s in range(count)])


def nn(a, b):
    return jnp.dot(a, b, preferred_element_type=F32)


def nt(a, b):
    return lax.dot_general(a, b, (((1,), (1,)), ((), ())), preferred_element_type=F32)


def tn(a, b):
    return lax.dot_general(a, b, (((0,), (0,)), ((), ())), preferred_element_type=F32)


def pick_rows(chosen_ref, cand_ref):
    pairs, cands = chosen_ref.shape[0], cand_ref.shape[0]
    spots = lax.broadcasted_iota(jnp.int32, (pairs, cands), 1)
    return nn((spots == chosen_ref[...]).astype(BF16), cand_ref[...])


def text_kernel(chosen_ref, cand_ref, unit_ref, norm_ref):
    texts = pick_rows(chosen_ref, cand_ref)
    norm = jnp.sqrt(jnp.sum(texts * texts, axis=1, keepdims=True) + EPS)
    unit_ref[...] = (texts / norm).astype(BF16)
    norm_ref[...] = norm


def image_kernel(chosen_ref, cand_ref, out_ref):
    out_ref[...] = pick_rows(chosen_ref, cand_ref).astype(BF16)


def pair_kernel(blocks, spot_ref, mine_ref, there_ref, images_ref, cols_mine_ref, cols_other_ref, flat_ref, group_ref):
    pairs, depth = mine_ref.shape
    first = spot_ref[0] == 0
    images_ref[:pairs, :] = jnp.where(first, mine_ref[...], there_ref[...])
    images_ref[pairs:, :] = jnp.where(first, there_ref[...], mine_ref[...])
    flat_ref[...] = images_ref[...].astype(F32).T
    size = depth // blocks
    for block in range(blocks):
        place = block // 2 * size
        group_ref[block % 2, place:place + size, :] = flat_ref[block * size:(block + 1) * size, :]
    core = spot_ref[2]
    cols_mine_ref[...] = group_ref[core].astype(BF16)
    cols_other_ref[...] = group_ref[1 - core].astype(BF16)


def main_kernel(scal_ref, spot_ref, images_ref, mine_ref, other_ref, cols_ref, text_hbm, send_ref, back_ref, part_hbm,
                text_ref, part_ref, proj_ref, total_ref, in_sem, out_sem):
    load = pltpu.make_async_copy(text_hbm, text_ref, in_sem)
    load.start()
    temper, offset, factor = scal_ref[0], scal_ref[1], scal_ref[2]
    rows, width = proj_ref.shape
    first = spot_ref[2] == 0
    proj_mine, proj_other = nn(images_ref[...], mine_ref[...]), nn(images_ref[...], other_ref[...])
    proj_ref[:, :WIDE] = jnp.where(first, proj_mine, proj_other)
    proj_ref[:, WIDE:] = jnp.where(first, proj_other, proj_mine)[:, 2 * WIDE - width:]
    proj = proj_ref[...]
    norm = jnp.sqrt(jnp.sum(proj * proj, axis=1, keepdims=True) + EPS)
    unit = (proj / norm).astype(BF16)
    pair = rows // 2
    row_id = lax.broadcasted_iota(jnp.int32, (rows, CHUNK), 0) - spot_ref[0]
    col_id = lax.broadcasted_iota(jnp.int32, (rows, CHUNK), 1) - spot_ref[1]
    inside = (row_id >= 0) & (row_id < pair)
    load.wait()
    stores = []
    for k in range(text_ref.shape[0] // CHUNK):
        block = pl.ds(k * CHUNK, CHUNK)
        text = text_ref[block, :]
        logits = temper * nt(unit, text) + offset
        sign = jnp.where(inside & (col_id + k * CHUNK == row_id), 1.0, -1.0)
        grad = (-factor * sign / (1.0 + jnp.exp(sign * logits))).astype(BF16)
        if k == 0:
            total_ref[...] = nn(grad, text)
        else:
            total_ref[...] += nn(grad, text)
        part_ref[block, :] = (temper * tn(grad, unit)).astype(BF16)
        store = pltpu.make_async_copy(part_ref.at[block], part_hbm.at[block], out_sem.at[k])
        store.start()
        stores.append(store)
    image_back = temper * total_ref[...]
    unit_float = unit.astype(F32)
    radial = jnp.sum(unit_float * image_back, axis=1, keepdims=True)
    back = ((image_back - unit_float * radial) / norm).astype(BF16)
    back_ref[...] = back
    send_ref[...] = nn(cols_ref[...], back).astype(BF16)
    for store in stores:
        store.wait()


def place_kernel(chosen_ref, back_ref, unit_ref, norm_ref, out_ref):
    back = back_ref[...].astype(F32)
    unit = unit_ref[...].astype(F32)
    radial = jnp.sum(unit * back, axis=1, keepdims=True)
    rows = (back - unit * radial) / norm_ref[...]
    spots = lax.broadcasted_iota(jnp.int32, (out_ref.shape[0], rows.shape[0]), 0)
    here = (spots == chosen_ref[...]).astype(F32)
    out_ref[...] = jnp.dot(here, rows, precision=lax.Precision.HIGHEST, preferred_element_type=F32)


def call(kernel, outs, in_specs, out_specs, scratch=(), cost=0):
    return pl.pallas_call(
        kernel,
        out_shape=tuple(jax.ShapeDtypeStruct(shape, dtype) for shape, dtype in outs),
        in_specs=in_specs,
        out_specs=out_specs,
        scratch_shapes=list(scratch),
        compiler_params=PARAMS,
        cost_estimate=pl.CostEstimate(flops=cost, bytes_accessed=2_000_000, transcendentals=0),
    )


def shards(image_cand, text_cand, selection, head_weight, logit_temp, logit_offset, loss_scale):
    pairs = selection.shape[0]
    cands, depth = image_cand.shape
    own_rows, width = head_weight.shape
    rows = 2 * pairs
    n_y, n_x = lax.axis_size("y"), lax.axis_size("x")
    my_zl, my_y, core = (lax.axis_index(a) for a in ("zl", "y", "c"))
    total = pairs * lax.axis_size(ALL)
    spot = jnp.stack([my_zl * pairs, my_y * pairs, core])
    scalars = jnp.stack([logit_temp[0], logit_offset[0], loss_scale[0] / total])

    text_unit, txt_norm = call(
        text_kernel, [((pairs, width), BF16), ((pairs, 1), F32)], [VMEM, VMEM], (VMEM, VMEM), cost=2 * pairs * cands * width,
    )(selection[:, None], text_cand)
    text_all = lax.all_gather(text_unit, "y", axis=0, tiled=True)

    both = lax.all_gather(head_weight, "c", axis=0, tiled=True)
    part = lax.dynamic_slice(both, (0, core * (width - WIDE)), (2 * own_rows, WIDE))
    slab = lax.all_gather(part, "zh", axis=0, tiled=True)
    (picked,) = call(
        image_kernel, [((pairs, depth), BF16)], [VMEM, VMEM], (VMEM,), cost=2 * pairs * cands * depth,
    )(selection[:, None], image_cand)
    slab, picked = lax.optimization_barrier((slab, picked))
    there = hop(picked, "zl", 1)
    slabs = lax.all_to_all(jnp.broadcast_to(slab[None], (n_x,) + slab.shape), "x", 0, 0)
    mine = slabs.reshape(depth, WIDE)
    other = hop(mine, "c", 1)

    blocks = depth // own_rows
    images, cols_mine, cols_other = call(
        lambda *refs: pair_kernel(blocks, *refs),
        [((rows, depth), BF16), ((depth // 2, rows), BF16), ((depth // 2, rows), BF16)],
        [SMEM, VMEM, VMEM], (VMEM, VMEM, VMEM),
        [pltpu.VMEM((depth, rows), F32), pltpu.VMEM((2, depth // 2, rows), F32)],
    )(spot, picked, there)

    send, proj_back, text_part = call(
        main_kernel,
        [((depth // 2, width), BF16), ((rows, width), BF16), ((n_y * pairs, width), BF16)],
        [SMEM, SMEM, VMEM, VMEM, VMEM, VMEM, ANY], (VMEM, VMEM, ANY),
        [pltpu.VMEM((n_y * pairs, width), BF16), pltpu.VMEM((n_y * pairs, width), BF16),
         pltpu.VMEM((rows, width), F32), pltpu.VMEM((rows, width), F32),
         pltpu.SemaphoreType.DMA, pltpu.SemaphoreType.DMA((n_y * pairs // CHUNK,))],
        cost=6 * rows * n_y * pairs * width,
    )(scalars, spot, images, mine, other, cols_other, text_all)

    text_back = lax.psum_scatter(text_part.reshape(n_y, pairs, width), "y", scatter_dimension=0)
    got = hop(send, "c", 1)
    head = nn(cols_mine, proj_back) + got.astype(F32)

    def spread(values, axis):
        count = lax.axis_size(axis)
        parts = values.astype(BF16).reshape(count, values.shape[0] // count, values.shape[1])
        return jnp.sum(lax.all_to_all(parts, axis, 0, 0).astype(F32), axis=0)

    head = spread(head, "x")
    head = spread(head, ("zh", "zl"))
    copies = jnp.broadcast_to(head.astype(BF16)[None], (n_y,) + head.shape)
    head = jnp.sum(lax.all_to_all(copies, "y", 0, 0).astype(F32), axis=0)
    head_grad = lax.all_gather(head, "zl", axis=0, tiled=True)

    (text_grad,) = call(
        place_kernel, [((cands, width), F32)], [VMEM] * 4, (VMEM,), cost=12 * cands * pairs * width,
    )(selection[None, :], text_back, text_unit, txt_norm)
    return head_grad, text_grad


def solution(mesh):
    devices = mesh.devices
    fine = Mesh(devices.reshape(2, devices.shape[0] // 2, 4, devices.shape[1] // 8, 2), ALL)
    return jax.shard_map(
        shards,
        mesh=fine,
        in_specs=(P(ALL, None), P(ALL, None), P(ALL), P(("x", "zh", "c"), None), P(), P(), P()),
        out_specs=(P(("x", "zh", "c"), None), P(ALL, None)),
        check_vma=False,
    )
```

```python
import jax
import jax.numpy as jnp
from jax import lax
from jax.experimental import pallas as pl
from jax.experimental.pallas import tpu as pltpu
from jax.sharding import Mesh, PartitionSpec as P

EPS = 1e-06
ALL = ("zl", "y", "x", "zh", "c")
WIDE = 640
CHUNK = 256
VMEM = pl.BlockSpec(memory_space=pltpu.VMEM)
SMEM = pl.BlockSpec(memory_space=pltpu.SMEM)
HBM = pl.BlockSpec(memory_space=pltpu.HBM)
LANES = 128
PARAMS = pltpu.CompilerParams(vmem_limit_bytes=40 * 1024 * 1024)
F32, BF16 = jnp.float32, jnp.bfloat16


def hop(value, axis, steps):
    count = lax.axis_size(axis)
    return lax.ppermute(value, axis, [(s, (s + steps) % count) for s in range(count)])


def nn(a, b):
    return jnp.dot(a, b, preferred_element_type=F32)


def nt(a, b):
    return lax.dot_general(a, b, (((1,), (1,)), ((), ())), preferred_element_type=F32)


def tn(a, b):
    return lax.dot_general(a, b, (((0,), (0,)), ((), ())), preferred_element_type=F32)


def pick_rows(chosen_ref, cand_ref):
    pairs, cands = chosen_ref.shape[1], cand_ref.shape[0]
    spots = lax.broadcasted_iota(jnp.int32, (cands, pairs), 0)
    return tn((spots == chosen_ref[...]).astype(BF16), cand_ref[...])


def text_kernel(chosen_ref, cand_ref, unit_ref, norm_ref):
    texts = pick_rows(chosen_ref, cand_ref)
    norm = jnp.sqrt(jnp.sum(texts * texts, axis=1, keepdims=True) + EPS)
    unit_ref[...] = (texts / norm).astype(BF16)
    norm_ref[...] = norm


def image_kernel(chosen_ref, cand_ref, out_ref):
    out_ref[...] = pick_rows(chosen_ref, cand_ref).astype(BF16)


def pair_kernel(blocks, spot_ref, mine_ref, there_ref, images_ref, cols_mine_ref, cols_other_ref, flat_ref, group_ref):
    pairs, depth = mine_ref.shape
    first = spot_ref[0] == 0
    images_ref[:pairs, :] = jnp.where(first, mine_ref[...], there_ref[...])
    images_ref[pairs:, :] = jnp.where(first, there_ref[...], mine_ref[...])
    flat_ref[...] = images_ref[...].astype(F32).T
    size = depth // blocks
    for block in range(blocks):
        place = block // 2 * size
        group_ref[block % 2, place:place + size, :] = flat_ref[block * size:(block + 1) * size, :]
    core = spot_ref[2]
    cols_mine_ref[...] = group_ref[core].astype(BF16)
    cols_other_ref[...] = group_ref[1 - core].astype(BF16)


def half_kernel(images_ref, mine_ref, out_ref):
    out_ref[...] = nn(images_ref[...], mine_ref[...])


def main_kernel(scal_ref, spot_ref, images_ref, half_ref, other_ref, cols_ref, text_hbm, send_ref, back_ref, unit_ref, grad_ref,
                text_ref, proj_ref, total_ref, sem):
    load = pltpu.make_async_copy(text_hbm, text_ref, sem)
    load.start()
    temper, offset, factor = scal_ref[0], scal_ref[1], scal_ref[2]
    rows, width = proj_ref.shape
    first = spot_ref[2] == 0
    proj_mine, proj_other = half_ref[...], nn(images_ref[...], other_ref[...])
    proj_ref[:, :WIDE] = jnp.where(first, proj_mine, proj_other)
    proj_ref[:, WIDE:] = jnp.where(first, proj_other, proj_mine)[:, 2 * WIDE - width:]
    proj = proj_ref[...]
    norm = jnp.sqrt(jnp.sum(proj * proj, axis=1, keepdims=True) + EPS)
    unit = (proj / norm).astype(BF16)
    unit_ref[...] = unit
    pair = rows // 2
    row_id = lax.broadcasted_iota(jnp.int32, (rows, CHUNK), 0) - spot_ref[0]
    col_id = lax.broadcasted_iota(jnp.int32, (rows, CHUNK), 1) - spot_ref[1]
    inside = (row_id >= 0) & (row_id < pair)
    load.wait()
    for k in range(text_ref.shape[0] // CHUNK):
        block = slice(k * CHUNK, (k + 1) * CHUNK)
        text = text_ref[block, :]
        logits = temper * nt(unit, text) + offset
        sign = jnp.where(inside & (col_id + k * CHUNK == row_id), 1.0, -1.0)
        grad = (-factor * sign / (1.0 + jnp.exp(sign * logits))).astype(BF16)
        grad_ref[:, block] = grad
        if k == 0:
            total_ref[...] = nn(grad, text)
        else:
            total_ref[...] += nn(grad, text)
    image_back = temper * total_ref[...]
    unit_float = unit.astype(F32)
    radial = jnp.sum(unit_float * image_back, axis=1, keepdims=True)
    back = ((image_back - unit_float * radial) / norm).astype(BF16)
    back_ref[...] = back
    send_ref[...] = nn(cols_ref[...], back).astype(BF16)


def part_kernel(scal_ref, grad_ref, unit_ref, part_hbm, part_ref, sem):
    unit = unit_ref[...]
    stores = []
    for k in range(part_ref.shape[0] // CHUNK):
        block = pl.ds(k * CHUNK, CHUNK)
        part_ref[block, :] = (scal_ref[0] * tn(grad_ref[:, k * CHUNK:(k + 1) * CHUNK], unit)).astype(BF16)
        store = pltpu.make_async_copy(part_ref.at[block], part_hbm.at[block], sem.at[k])
        store.start()
        stores.append(store)
    for store in stores:
        store.wait()


def fold_kernel(came_ref, out_ref, sum_ref, flat_ref):
    total = came_ref[0].astype(F32)
    for k in range(1, came_ref.shape[0]):
        total += came_ref[k].astype(F32)
    sum_ref[...] = total
    flat_ref[...] = jnp.zeros_like(flat_ref)
    pieces = flat_ref.shape[0]
    size = sum_ref.shape[0] // pieces
    for p in range(pieces):
        for t in range(sum_ref.shape[1] // LANES):
            flat_ref[p, t * size:(t + 1) * size, :] = sum_ref[p * size:(p + 1) * size, t * LANES:(t + 1) * LANES]
    out_ref[...] = flat_ref[...].astype(BF16)


def unfold_kernel(came_ref, out_ref, sum_ref):
    total = came_ref[0].astype(F32)
    for k in range(1, came_ref.shape[0]):
        total += came_ref[k].astype(F32)
    sum_ref[...] = total
    size = out_ref.shape[0]
    for t in range(out_ref.shape[1] // LANES):
        out_ref[:, t * LANES:(t + 1) * LANES] = sum_ref[t * size:(t + 1) * size, :]


def place_kernel(chosen_ref, back_ref, unit_ref, norm_ref, out_ref):
    back = back_ref[...].astype(F32)
    unit = unit_ref[...].astype(F32)
    radial = jnp.sum(unit * back, axis=1, keepdims=True)
    rows = (back - unit * radial) / norm_ref[...]
    spots = lax.broadcasted_iota(jnp.int32, (out_ref.shape[0], rows.shape[0]), 0)
    here = (spots == chosen_ref[...]).astype(F32)
    out_ref[...] = jnp.dot(here, rows, precision=lax.Precision.HIGHEST, preferred_element_type=F32)


def call(kernel, outs, in_specs, out_specs, scratch=(), cost=0):
    return pl.pallas_call(
        kernel,
        out_shape=tuple(jax.ShapeDtypeStruct(shape, dtype) for shape, dtype in outs),
        in_specs=in_specs,
        out_specs=out_specs,
        scratch_shapes=list(scratch),
        compiler_params=PARAMS,
        cost_estimate=pl.CostEstimate(flops=cost, bytes_accessed=2_000_000, transcendentals=0),
    )


def shards(image_cand, text_cand, selection, head_weight, logit_temp, logit_offset, loss_scale):
    pairs = selection.shape[0]
    cands, depth = image_cand.shape
    own_rows, width = head_weight.shape
    rows = 2 * pairs
    n_y, n_x = lax.axis_size("y"), lax.axis_size("x")
    my_zl, my_y, core = (lax.axis_index(a) for a in ("zl", "y", "c"))
    total = pairs * lax.axis_size(ALL)
    spot = jnp.stack([my_zl * pairs, my_y * pairs, core])
    scalars = jnp.stack([logit_temp[0], logit_offset[0], loss_scale[0] / total])

    text_unit, txt_norm = call(
        text_kernel, [((pairs, width), BF16), ((pairs, 1), F32)], [VMEM, VMEM], (VMEM, VMEM), cost=2 * pairs * cands * width,
    )(selection[None, :], text_cand)
    text_all = lax.all_gather(text_unit, "y", axis=0, tiled=True)

    (picked,) = call(
        image_kernel, [((pairs, depth), BF16)], [VMEM, VMEM], (VMEM,), cost=2 * pairs * cands * depth,
    )(selection[None, :], image_cand)
    there = hop(picked, "zl", 1)

    both = lax.all_gather(head_weight, "c", axis=0, tiled=True)
    part = lax.dynamic_slice(both, (0, core * (width - WIDE)), (2 * own_rows, WIDE))
    slab = lax.all_gather(part, "zh", axis=0, tiled=True)
    slab, there = lax.optimization_barrier((slab, there))
    slabs = lax.all_to_all(jnp.broadcast_to(slab[None], (n_x,) + slab.shape), "x", 0, 0)
    mine = slabs.reshape(depth, WIDE)
    other = hop(mine, "c", 1)

    blocks = depth // own_rows
    images, cols_mine, cols_other = call(
        lambda *refs: pair_kernel(blocks, *refs),
        [((rows, depth), BF16), ((depth // 2, rows), BF16), ((depth // 2, rows), BF16)],
        [SMEM, VMEM, VMEM], (VMEM, VMEM, VMEM),
        [pltpu.VMEM((depth, rows), F32), pltpu.VMEM((2, depth // 2, rows), F32)],
    )(spot, picked, there)

    (half,) = call(
        half_kernel, [((rows, WIDE), F32)], [VMEM, VMEM], (VMEM,), cost=2 * rows * depth * WIDE,
    )(images, mine)
    send, proj_back, image_unit, grad_tile = call(
        main_kernel,
        [((depth // 2, width), BF16), ((rows, width), BF16), ((rows, width), BF16), ((rows, n_y * pairs), BF16)],
        [SMEM, SMEM, VMEM, VMEM, VMEM, VMEM, HBM], (VMEM,) * 4,
        [pltpu.VMEM((n_y * pairs, width), BF16), pltpu.VMEM((rows, width), F32), pltpu.VMEM((rows, width), F32),
         pltpu.SemaphoreType.DMA],
        cost=5 * rows * n_y * pairs * width,
    )(scalars, spot, images, half, other, cols_other, text_all)
    (text_part,) = call(
        part_kernel, [((n_y * pairs, width), BF16)], [SMEM, VMEM, VMEM], (HBM,),
        [pltpu.VMEM((n_y * pairs, width), BF16), pltpu.SemaphoreType.DMA((n_y * pairs // CHUNK,))],
        cost=2 * rows * n_y * pairs * width,
    )(scalars, grad_tile, image_unit)

    text_back = lax.psum_scatter(text_part.reshape(n_y, pairs, width), "y", scatter_dimension=0)
    got = hop(send, "c", 1)
    head = nn(cols_mine, proj_back) + got.astype(F32)

    share = depth // 2 // n_x
    came = lax.all_to_all(head.astype(BF16).reshape(n_x, share, width), "x", 0, 0)
    n_z = lax.axis_size(("zh", "zl"))
    piece = share // n_z
    strips = piece * (width // LANES)
    strips += -strips % 8
    (folded,) = call(
        fold_kernel, [((n_z, strips, LANES), BF16)], [VMEM], (VMEM,),
        [pltpu.VMEM((share, width), F32), pltpu.VMEM((n_z, strips, LANES), F32)],
    )(came)
    came = lax.all_to_all(folded, ("zh", "zl"), 0, 0)
    head = jnp.sum(came.astype(F32), axis=0).astype(BF16)
    came = lax.all_to_all(jnp.broadcast_to(head[None], (n_y,) + head.shape), "y", 0, 0)
    (head,) = call(unfold_kernel, [((piece, width), F32)], [VMEM], (VMEM,), [pltpu.VMEM((strips, LANES), F32)])(came)

    (text_grad,) = call(
        place_kernel, [((cands, width), F32)], [VMEM] * 4, (VMEM,), cost=12 * cands * pairs * width,
    )(selection[None, :], text_back, text_unit, txt_norm)
    head, text_grad = lax.optimization_barrier((head, text_grad))
    head_grad = lax.all_gather(head, "zl", axis=0, tiled=True)
    return head_grad, text_grad


def solution(mesh):
    devices = mesh.devices
    fine = Mesh(devices.reshape(2, devices.shape[0] // 2, 4, devices.shape[1] // 8, 2), ALL)
    return jax.shard_map(
        shards,
        mesh=fine,
        in_specs=(P(ALL, None), P(ALL, None), P(ALL), P(("x", "zh", "c"), None), P(), P(), P()),
        out_specs=(P(("x", "zh", "c"), None), P(ALL, None)),
        check_vma=False,
    )
```

```python
import jax
import jax.numpy as jnp
from jax import lax
from jax.experimental import pallas as pl
from jax.experimental.pallas import tpu as pltpu
from jax.sharding import Mesh, PartitionSpec as P

EPS = 1e-06
ALL = ("zl", "y", "x", "zh", "c")
WIDE = 640
CHUNK = 256
VMEM = pl.BlockSpec(memory_space=pltpu.VMEM)
SMEM = pl.BlockSpec(memory_space=pltpu.SMEM)
HBM = pl.BlockSpec(memory_space=pltpu.HBM)
LANES = 128
PARAMS = pltpu.CompilerParams(vmem_limit_bytes=40 * 1024 * 1024)
F32, BF16 = jnp.float32, jnp.bfloat16


def hop(value, axis, steps):
    count = lax.axis_size(axis)
    return lax.ppermute(value, axis, [(s, (s + steps) % count) for s in range(count)])


def nn(a, b):
    return jnp.dot(a, b, preferred_element_type=F32)


def nt(a, b):
    return lax.dot_general(a, b, (((1,), (1,)), ((), ())), preferred_element_type=F32)


def tn(a, b):
    return lax.dot_general(a, b, (((0,), (0,)), ((), ())), preferred_element_type=F32)


def pick_rows(chosen_ref, cand_ref):
    pairs, cands = chosen_ref.shape[1], cand_ref.shape[0]
    spots = lax.broadcasted_iota(jnp.int32, (cands, pairs), 0)
    return tn((spots == chosen_ref[...]).astype(BF16), cand_ref[...])


def pick_kernel(chosen_ref, text_cand_ref, image_cand_ref, unit_ref, norm_ref, picked_ref):
    texts = pick_rows(chosen_ref, text_cand_ref)
    norm = jnp.sqrt(jnp.sum(texts * texts, axis=1, keepdims=True) + EPS)
    unit_ref[...] = (texts / norm).astype(BF16)
    norm_ref[...] = norm
    picked_ref[...] = pick_rows(chosen_ref, image_cand_ref).astype(BF16)


def pair_kernel(blocks, spot_ref, mine_ref, there_ref, images_ref, cols_mine_ref, cols_other_ref, flat_ref, group_ref):
    pairs, depth = mine_ref.shape
    first = spot_ref[0] == 0
    images_ref[:pairs, :] = jnp.where(first, mine_ref[...], there_ref[...])
    images_ref[pairs:, :] = jnp.where(first, there_ref[...], mine_ref[...])
    flat_ref[...] = images_ref[...].astype(F32).T
    size = depth // blocks
    for block in range(blocks):
        place = block // 2 * size
        group_ref[block % 2, place:place + size, :] = flat_ref[block * size:(block + 1) * size, :]
    core = spot_ref[2]
    cols_mine_ref[...] = group_ref[core].astype(BF16)
    cols_other_ref[...] = group_ref[1 - core].astype(BF16)


def half_kernel(images_ref, mine_ref, out_ref):
    out_ref[...] = nn(images_ref[...], mine_ref[...])


def main_kernel(scal_ref, spot_ref, images_ref, half_ref, other_ref, cols_ref, text_ref, send_ref, back_ref, unit_ref, grad_ref,
                proj_ref):
    temper, offset, factor = scal_ref[0], scal_ref[1], scal_ref[2]
    rows, width = proj_ref.shape
    first = spot_ref[2] == 0
    proj_mine, proj_other = half_ref[...], nn(images_ref[...], other_ref[...])
    proj_ref[:, :WIDE] = jnp.where(first, proj_mine, proj_other)
    proj_ref[:, WIDE:] = jnp.where(first, proj_other, proj_mine)[:, 2 * WIDE - width:]
    proj = proj_ref[...]
    norm = jnp.sqrt(jnp.sum(proj * proj, axis=1, keepdims=True) + EPS)
    unit = (proj / norm).astype(BF16)
    unit_ref[...] = unit
    pair = rows // 2
    row_id = lax.broadcasted_iota(jnp.int32, (rows, CHUNK), 0) - spot_ref[0]
    col_id = lax.broadcasted_iota(jnp.int32, (rows, CHUNK), 1) - spot_ref[1]
    inside = (row_id >= 0) & (row_id < pair)
    for k in range(text_ref.shape[0] // CHUNK):
        block = slice(k * CHUNK, (k + 1) * CHUNK)
        text = text_ref[block, :]
        logits = temper * nt(unit, text) + offset
        sign = jnp.where(inside & (col_id + k * CHUNK == row_id), 1.0, -1.0)
        grad = (-factor * sign / (1.0 + jnp.exp(sign * logits))).astype(BF16)
        grad_ref[:, block] = grad
    image_back = temper * nn(grad_ref[...], text_ref[...])
    unit_float = unit.astype(F32)
    radial = jnp.sum(unit_float * image_back, axis=1, keepdims=True)
    back = ((image_back - unit_float * radial) / norm).astype(BF16)
    back_ref[...] = back
    send_ref[...] = nn(cols_ref[...], back).astype(BF16)


def part_kernel(scal_ref, grad_ref, unit_ref, part_hbm, part_ref, sem):
    unit = unit_ref[...]
    stores = []
    for k in range(part_ref.shape[0] // CHUNK):
        block = pl.ds(k * CHUNK, CHUNK)
        part_ref[block, :] = (scal_ref[0] * tn(grad_ref[:, k * CHUNK:(k + 1) * CHUNK], unit)).astype(BF16)
        store = pltpu.make_async_copy(part_ref.at[block], part_hbm.at[block], sem.at[k])
        store.start()
        stores.append(store)
    for store in stores:
        store.wait()


def fold_kernel(came_ref, out_ref, sum_ref, flat_ref):
    total = came_ref[0].astype(F32)
    for k in range(1, came_ref.shape[0]):
        total += came_ref[k].astype(F32)
    sum_ref[...] = total
    flat_ref[...] = jnp.zeros_like(flat_ref)
    pieces = flat_ref.shape[0]
    size = sum_ref.shape[0] // pieces
    for p in range(pieces):
        for t in range(sum_ref.shape[1] // LANES):
            flat_ref[p, t * size:(t + 1) * size, :] = sum_ref[p * size:(p + 1) * size, t * LANES:(t + 1) * LANES]
    out_ref[...] = flat_ref[...].astype(BF16)


def unfold_kernel(came_ref, out_ref, sum_ref):
    total = came_ref[0].astype(F32)
    for k in range(1, came_ref.shape[0]):
        total += came_ref[k].astype(F32)
    sum_ref[...] = total
    size = out_ref.shape[0]
    for t in range(out_ref.shape[1] // LANES):
        out_ref[:, t * LANES:(t + 1) * LANES] = sum_ref[t * size:(t + 1) * size, :]


def place_kernel(chosen_ref, back_ref, unit_ref, norm_ref, out_ref):
    back = back_ref[...].astype(F32)
    unit = unit_ref[...].astype(F32)
    radial = jnp.sum(unit * back, axis=1, keepdims=True)
    rest = (back - unit * radial) / norm_ref[...]
    spots = lax.broadcasted_iota(jnp.int32, (out_ref.shape[0], rest.shape[0]), 0)
    here = (spots == chosen_ref[...]).astype(BF16)
    placed = None
    for _ in range(3):
        part = rest.astype(BF16)
        rest = rest - part.astype(F32)
        placed = nn(here, part) if placed is None else placed + nn(here, part)
    out_ref[...] = placed


def call(kernel, outs, in_specs, out_specs, scratch=(), cost=0):
    return pl.pallas_call(
        kernel,
        out_shape=tuple(jax.ShapeDtypeStruct(shape, dtype) for shape, dtype in outs),
        in_specs=in_specs,
        out_specs=out_specs,
        scratch_shapes=list(scratch),
        compiler_params=PARAMS,
        cost_estimate=pl.CostEstimate(flops=cost, bytes_accessed=2_000_000, transcendentals=0),
    )


def shards(image_cand, text_cand, selection, head_weight, logit_temp, logit_offset, loss_scale):
    pairs = selection.shape[0]
    cands, depth = image_cand.shape
    own_rows, width = head_weight.shape
    rows = 2 * pairs
    n_y, n_x = lax.axis_size("y"), lax.axis_size("x")
    my_zl, my_y, core = (lax.axis_index(a) for a in ("zl", "y", "c"))
    total = pairs * lax.axis_size(ALL)
    spot = jnp.stack([my_zl * pairs, my_y * pairs, core])
    scalars = jnp.stack([logit_temp[0], logit_offset[0], loss_scale[0] / total])

    both = lax.all_gather(head_weight, "c", axis=0, tiled=True)
    both, selection = lax.optimization_barrier((both, selection))
    chosen = selection[None, :]
    text_unit, txt_norm, picked = call(
        pick_kernel, [((pairs, width), BF16), ((pairs, 1), F32), ((pairs, depth), BF16)], [VMEM] * 3, (VMEM,) * 3,
        cost=2 * pairs * cands * (width + depth),
    )(chosen, text_cand, image_cand)
    text_all = lax.all_gather(text_unit, "y", axis=0, tiled=True)
    there = hop(picked, "zl", 1)

    part = lax.dynamic_slice(both, (0, core * (width - WIDE)), (2 * own_rows, WIDE))
    slab = lax.all_gather(part, "zh", axis=0, tiled=True)
    slab, there = lax.optimization_barrier((slab, there))
    slabs = lax.all_to_all(jnp.broadcast_to(slab[None], (n_x,) + slab.shape), "x", 0, 0)
    mine = slabs.reshape(depth, WIDE)
    other = hop(mine, "c", 1)

    there, text_all = lax.optimization_barrier((there, text_all))
    blocks = depth // own_rows
    images, cols_mine, cols_other = call(
        lambda *refs: pair_kernel(blocks, *refs),
        [((rows, depth), BF16), ((depth // 2, rows), BF16), ((depth // 2, rows), BF16)],
        [SMEM, VMEM, VMEM], (VMEM, VMEM, VMEM),
        [pltpu.VMEM((depth, rows), F32), pltpu.VMEM((2, depth // 2, rows), F32)],
    )(spot, picked, there)

    (half,) = call(
        half_kernel, [((rows, WIDE), F32)], [VMEM, VMEM], (VMEM,), cost=2 * rows * depth * WIDE,
    )(images, mine)
    send, proj_back, image_unit, grad_tile = call(
        main_kernel,
        [((depth // 2, width), BF16), ((rows, width), BF16), ((rows, width), BF16), ((rows, n_y * pairs), BF16)],
        [SMEM, SMEM] + [VMEM] * 5, (VMEM,) * 4, [pltpu.VMEM((rows, width), F32)],
        cost=5 * rows * n_y * pairs * width,
    )(scalars, spot, images, half, other, cols_other, text_all)
    got = hop(send, "c", 1)
    got, grad_tile = lax.optimization_barrier((got, grad_tile))
    head = (nn(cols_mine, proj_back) + got.astype(F32)).astype(BF16)
    (text_part,) = call(
        part_kernel, [((n_y * pairs, width), BF16)], [SMEM, VMEM, VMEM], (HBM,),
        [pltpu.VMEM((n_y * pairs, width), BF16), pltpu.SemaphoreType.DMA((n_y * pairs // CHUNK,))],
        cost=2 * rows * n_y * pairs * width,
    )(scalars, grad_tile, image_unit)

    head, text_part = lax.optimization_barrier((head, text_part))
    text_back = lax.psum_scatter(text_part.reshape(n_y, pairs, width), "y", scatter_dimension=0)
    share = depth // 2 // n_x
    came = lax.all_to_all(head.reshape(n_x, share, width), "x", 0, 0)
    n_z = lax.axis_size(("zh", "zl"))
    piece = share // n_z
    strips = piece * (width // LANES)
    strips += -strips % 8
    (folded,) = call(
        fold_kernel, [((n_z, strips, LANES), BF16)], [VMEM], (VMEM,),
        [pltpu.VMEM((share, width), F32), pltpu.VMEM((n_z, strips, LANES), F32)],
    )(came)
    came = lax.all_to_all(folded, ("zh", "zl"), 0, 0)
    head = jnp.sum(came.astype(F32), axis=0).astype(BF16)
    came = lax.all_to_all(jnp.broadcast_to(head[None], (n_y,) + head.shape), "y", 0, 0)
    (head,) = call(unfold_kernel, [((piece, width), F32)], [VMEM], (VMEM,), [pltpu.VMEM((strips, LANES), F32)])(came)

    there = hop(head, "zl", 1)
    (text_grad,) = call(
        place_kernel, [((cands, width), F32)], [VMEM] * 4, (VMEM,), cost=6 * cands * pairs * width,
    )(chosen, text_back, text_unit, txt_norm)
    there, text_grad = lax.optimization_barrier((there, text_grad))
    head_grad = jnp.concatenate([jnp.where(my_zl == 0, head, there), jnp.where(my_zl == 0, there, head)], axis=0)
    return head_grad, text_grad


def solution(mesh):
    devices = mesh.devices
    fine = Mesh(devices.reshape(2, devices.shape[0] // 2, 4, devices.shape[1] // 8, 2), ALL)
    return jax.shard_map(
        shards,
        mesh=fine,
        in_specs=(P(ALL, None), P(ALL, None), P(ALL), P(("x", "zh", "c"), None), P(), P(), P()),
        out_specs=(P(("x", "zh", "c"), None), P(ALL, None)),
        check_vma=False,
    )
```

```python
import jax
import jax.numpy as jnp
from jax import lax
from jax.experimental import pallas as pl
from jax.experimental.pallas import tpu as pltpu
from jax.sharding import Mesh, PartitionSpec as P

EPS = 1e-06
ALL = ("zl", "y", "x", "zh", "c")
PADDED = 40
CHUNK = 256
VMEM = pl.BlockSpec(memory_space=pltpu.VMEM)
SMEM = pl.BlockSpec(memory_space=pltpu.SMEM)
HBM = pl.BlockSpec(memory_space=pltpu.HBM)
LANES = 128
LIMIT = 40 * 1024 * 1024
WHOLE = 61 * 1024 * 1024
F32, BF16 = jnp.float32, jnp.bfloat16


def hop(value, axis, steps):
    count = lax.axis_size(axis)
    return lax.ppermute(value, axis, [(s, (s + steps) % count) for s in range(count)])


def nn(a, b):
    return jnp.dot(a, b, preferred_element_type=F32)


def nt(a, b):
    return lax.dot_general(a, b, (((1,), (1,)), ((), ())), preferred_element_type=F32)


def tn(a, b):
    return lax.dot_general(a, b, (((0,), (0,)), ((), ())), preferred_element_type=F32)


def pick_rows(chosen, cands):
    spots = lax.broadcasted_iota(jnp.int32, (cands.shape[0], chosen.shape[1]), 0)
    return tn((spots == chosen).astype(BF16), cands)


def text_kernel(chosen_hbm, cand_hbm, unit_ref, norm_ref, chosen_ref, cand_ref, sem):
    loads = [pltpu.make_async_copy(chosen_hbm, chosen_ref, sem.at[0]), pltpu.make_async_copy(cand_hbm, cand_ref, sem.at[1])]
    for load in loads:
        load.start()
    for load in loads:
        load.wait()
    texts = pick_rows(chosen_ref[...], cand_ref[...])
    norm = jnp.sqrt(jnp.sum(texts * texts, axis=1, keepdims=True) + EPS)
    unit_ref[...] = (texts / norm).astype(BF16)
    norm_ref[...] = norm


def image_kernel(chosen_hbm, cand_hbm, out_ref, chosen_ref, cand_ref, sem):
    loads = [pltpu.make_async_copy(chosen_hbm, chosen_ref, sem.at[0]), pltpu.make_async_copy(cand_hbm, cand_ref, sem.at[1])]
    for load in loads:
        load.start()
    for load in loads:
        load.wait()
    out_ref[...] = pick_rows(chosen_ref[...], cand_ref[...]).astype(BF16)


def pair_kernel(size, spot_ref, mine_ref, there_ref, deep_mine_ref, deep_other_ref, cols_mine_ref, cols_other_ref,
                flat_ref, group_ref, deep_ref):
    pairs, depth = mine_ref.shape
    first = spot_ref[0] == 0
    mine, there = mine_ref[...].astype(F32).T, there_ref[...].astype(F32).T
    flat_ref[:, :pairs] = jnp.where(first, mine, there)
    flat_ref[:, pairs:] = jnp.where(first, there, mine)
    deep_ref[...] = jnp.zeros_like(deep_ref)
    for block in range(depth // size):
        core, place = block % 2, block // 2
        rows = flat_ref[block * size:(block + 1) * size, :]
        group_ref[core, place * size:(place + 1) * size, :] = rows
        deep_ref[core, place * PADDED:place * PADDED + size, :] = rows
    core = spot_ref[2]
    cols_mine_ref[...] = group_ref[core].astype(BF16)
    cols_other_ref[...] = group_ref[1 - core].astype(BF16)
    deep_mine_ref[...] = deep_ref[core].T.astype(BF16)
    deep_other_ref[...] = deep_ref[1 - core].T.astype(BF16)


def half_kernel(deep_ref, weight_ref, out_ref):
    out_ref[...] = nn(deep_ref[...], weight_ref[...])


def main_kernel(scal_ref, spot_ref, deep_ref, half_ref, weight_ref, cols_ref, text_ref, send_ref, back_ref, unit_ref, grad_ref):
    temper, offset, factor = scal_ref[0], scal_ref[1], scal_ref[2]
    proj = half_ref[...] + nn(deep_ref[...], weight_ref[...])
    rows = proj.shape[0]
    norm = jnp.sqrt(jnp.sum(proj * proj, axis=1, keepdims=True) + EPS)
    unit = (proj / norm).astype(BF16)
    unit_ref[...] = unit
    pair = rows // 2
    row_id = lax.broadcasted_iota(jnp.int32, (rows, CHUNK), 0) - spot_ref[0]
    col_id = lax.broadcasted_iota(jnp.int32, (rows, CHUNK), 1) - spot_ref[1]
    inside = (row_id >= 0) & (row_id < pair)
    for k in range(text_ref.shape[0] // CHUNK):
        block = slice(k * CHUNK, (k + 1) * CHUNK)
        text = text_ref[block, :]
        logits = temper * nt(unit, text) + offset
        sign = jnp.where(inside & (col_id + k * CHUNK == row_id), 1.0, -1.0)
        grad = (-factor * sign / (1.0 + jnp.exp(sign * logits))).astype(BF16)
        grad_ref[:, block] = grad
    image_back = temper * nn(grad_ref[...], text_ref[...])
    unit_float = unit.astype(F32)
    radial = jnp.sum(unit_float * image_back, axis=1, keepdims=True)
    back = ((image_back - unit_float * radial) / norm).astype(BF16)
    back_ref[...] = back
    send_ref[...] = nn(cols_ref[...], back).astype(BF16)


def part_kernel(grad_ref, unit_ref, part_hbm, part_ref, sem):
    unit = unit_ref[...]
    stores = []
    for k in range(part_ref.shape[0] // CHUNK):
        block = pl.ds(k * CHUNK, CHUNK)
        part_ref[block, :] = tn(grad_ref[:, k * CHUNK:(k + 1) * CHUNK], unit).astype(BF16)
        store = pltpu.make_async_copy(part_ref.at[block], part_hbm.at[block], sem.at[k])
        store.start()
        stores.append(store)
    for store in stores:
        store.wait()


def fold_kernel(came_ref, out_ref, sum_ref, flat_ref):
    total = came_ref[0].astype(F32)
    for k in range(1, came_ref.shape[0]):
        total += came_ref[k].astype(F32)
    sum_ref[...] = total
    flat_ref[...] = jnp.zeros_like(flat_ref)
    pieces = flat_ref.shape[0]
    size = sum_ref.shape[0] // pieces
    for p in range(pieces):
        for t in range(sum_ref.shape[1] // LANES):
            flat_ref[p, t * size:(t + 1) * size, :] = sum_ref[p * size:(p + 1) * size, t * LANES:(t + 1) * LANES]
    out_ref[...] = flat_ref[...].astype(BF16)


def unfold_kernel(came_ref, out_ref, sum_ref):
    total = came_ref[0].astype(F32)
    for k in range(1, came_ref.shape[0]):
        total += came_ref[k].astype(F32)
    sum_ref[...] = total
    size = out_ref.shape[0]
    for t in range(out_ref.shape[1] // LANES):
        out_ref[:, t * LANES:(t + 1) * LANES] = sum_ref[t * size:(t + 1) * size, :]


def place_kernel(scal_ref, chosen_ref, back_ref, unit_ref, norm_ref, out_ref):
    back = scal_ref[0] * back_ref[...].astype(F32)
    unit = unit_ref[...].astype(F32)
    radial = jnp.sum(unit * back, axis=1, keepdims=True)
    rest = (back - unit * radial) / norm_ref[...]
    spots = lax.broadcasted_iota(jnp.int32, (out_ref.shape[0], rest.shape[0]), 0)
    here = (spots == chosen_ref[...]).astype(BF16)
    placed = None
    for _ in range(3):
        part = rest.astype(BF16)
        rest = rest - part.astype(F32)
        placed = nn(here, part) if placed is None else placed + nn(here, part)
    out_ref[...] = placed


def call(kernel, outs, in_specs, out_specs, scratch=(), cost=0, limit=LIMIT):
    return pl.pallas_call(
        kernel,
        out_shape=tuple(jax.ShapeDtypeStruct(shape, dtype) for shape, dtype in outs),
        in_specs=in_specs,
        out_specs=out_specs,
        scratch_shapes=list(scratch),
        compiler_params=pltpu.CompilerParams(vmem_limit_bytes=limit),
        cost_estimate=pl.CostEstimate(flops=cost, bytes_accessed=2_000_000, transcendentals=0),
    )


def shards(image_cand, text_cand, selection, head_weight, logit_temp, logit_offset, loss_scale):
    pairs = selection.shape[0]
    cands, depth = image_cand.shape
    own_rows, width = head_weight.shape
    rows = 2 * pairs
    n_y, n_x = lax.axis_size("y"), lax.axis_size("x")
    my_zl, my_y, core = (lax.axis_index(a) for a in ("zl", "y", "c"))
    total = pairs * lax.axis_size(ALL)
    spot = jnp.stack([my_zl * pairs, my_y * pairs, core])
    scalars = jnp.stack([logit_temp[0], logit_offset[0], loss_scale[0] / total])

    chosen = selection[None, :]
    pick_scratch = [pltpu.VMEM((1, pairs), jnp.int32), pltpu.VMEM((cands, depth), BF16), pltpu.SemaphoreType.DMA((2,))]
    text_unit, txt_norm = call(
        text_kernel, [((pairs, width), BF16), ((pairs, 1), F32)], [HBM, HBM], (VMEM, VMEM), pick_scratch,
        cost=2 * pairs * cands * width, limit=WHOLE,
    )(chosen, text_cand)
    text_all = lax.all_gather(text_unit, "y", axis=0, tiled=True)

    part = jnp.pad(head_weight, ((0, PADDED - own_rows), (0, 0)))
    slab = lax.all_gather(part, "zh", axis=0, tiled=True)
    (picked,) = call(
        image_kernel, [((pairs, depth), BF16)], [HBM, HBM], (VMEM,), pick_scratch, cost=2 * pairs * cands * depth, limit=WHOLE,
    )(chosen, image_cand)
    slab, picked = lax.optimization_barrier((slab, picked))
    there = hop(picked, "zl", 1)
    slabs = lax.all_to_all(jnp.broadcast_to(slab[None], (n_x,) + slab.shape), "x", 0, 0)
    mine = slabs.reshape(n_x * slab.shape[0], width)
    mine, there = lax.optimization_barrier((mine, there))
    other = hop(mine, "c", 1)

    there, text_all = lax.optimization_barrier((there, text_all))
    deep = mine.shape[0]
    deep_mine, deep_other, cols_mine, cols_other = call(
        lambda *refs: pair_kernel(own_rows, *refs),
        [((rows, deep), BF16), ((rows, deep), BF16), ((depth // 2, rows), BF16), ((depth // 2, rows), BF16)],
        [SMEM, VMEM, VMEM], (VMEM,) * 4,
        [pltpu.VMEM((depth, rows), F32), pltpu.VMEM((2, depth // 2, rows), F32), pltpu.VMEM((2, deep, rows), F32)],
    )(spot, picked, there)
    (half,) = call(
        half_kernel, [((rows, width), F32)], [VMEM, VMEM], (VMEM,), cost=2 * rows * deep * width,
    )(deep_mine, mine)
    send, proj_back, image_unit, grad_tile = call(
        main_kernel,
        [((depth // 2, width), BF16), ((rows, width), BF16), ((rows, width), BF16), ((rows, n_y * pairs), BF16)],
        [SMEM, SMEM] + [VMEM] * 5, (VMEM,) * 4,
        cost=5 * rows * n_y * pairs * width,
    )(scalars, spot, deep_other, half, other, cols_other, text_all)
    got = hop(send, "c", 1)
    got, grad_tile = lax.optimization_barrier((got, grad_tile))
    head = (nn(cols_mine, proj_back) + got.astype(F32)).astype(BF16)
    (text_part,) = call(
        part_kernel, [((n_y * pairs, width), BF16)], [VMEM, VMEM], (HBM,),
        [pltpu.VMEM((n_y * pairs, width), BF16), pltpu.SemaphoreType.DMA((n_y * pairs // CHUNK,))],
        cost=2 * rows * n_y * pairs * width,
    )(grad_tile, image_unit)

    head, text_part = lax.optimization_barrier((head, text_part))
    text_back = lax.psum_scatter(text_part.reshape(n_y, pairs, width), "y", scatter_dimension=0)
    share = depth // 2 // n_x
    came = lax.all_to_all(head.reshape(n_x, share, width), "x", 0, 0)
    n_z = lax.axis_size(("zh", "zl"))
    piece = share // n_z
    strips = piece * (width // LANES)
    strips += -strips % 8
    (folded,) = call(
        fold_kernel, [((n_z, strips, LANES), BF16)], [VMEM], (VMEM,),
        [pltpu.VMEM((share, width), F32), pltpu.VMEM((n_z, strips, LANES), F32)],
    )(came)
    came = lax.all_to_all(folded, ("zh", "zl"), 0, 0)
    head = jnp.sum(came.astype(F32), axis=0).astype(BF16)
    came = lax.all_to_all(jnp.broadcast_to(head[None], (n_y,) + head.shape), "y", 0, 0)
    (head,) = call(unfold_kernel, [((piece, width), F32)], [VMEM], (VMEM,), [pltpu.VMEM((strips, LANES), F32)])(came)

    there = hop(head, "zl", 1)
    (text_grad,) = call(
        place_kernel, [((cands, width), F32)], [SMEM] + [VMEM] * 4, (VMEM,), cost=6 * cands * pairs * width,
    )(scalars, chosen, text_back, text_unit, txt_norm)
    there, text_grad = lax.optimization_barrier((there, text_grad))
    head_grad = jnp.concatenate([jnp.where(my_zl == 0, head, there), jnp.where(my_zl == 0, there, head)], axis=0)
    return head_grad, text_grad


def solution(mesh):
    devices = mesh.devices
    fine = Mesh(devices.reshape(2, devices.shape[0] // 2, 4, devices.shape[1] // 8, 2), ALL)
    return jax.shard_map(
        shards,
        mesh=fine,
        in_specs=(P(ALL, None), P(ALL, None), P(ALL), P(("x", "zh", "c"), None), P(), P(), P()),
        out_specs=(P(("x", "zh", "c"), None), P(ALL, None)),
        check_vma=False,
    )
```

```python
import jax
import jax.numpy as jnp
from jax import lax
from jax.experimental import pallas as pl
from jax.experimental.pallas import tpu as pltpu
from jax.sharding import Mesh, PartitionSpec as P

EPS = 1e-06
ALL = ("zl", "y", "x", "zh", "c")
PADDED = 40
CHUNK = 256
VMEM = pl.BlockSpec(memory_space=pltpu.VMEM)
SMEM = pl.BlockSpec(memory_space=pltpu.SMEM)
HBM = pl.BlockSpec(memory_space=pltpu.HBM)
LANES = 128
LIMIT = 8 * 1024 * 1024
ROOMY = 12 * 1024 * 1024
WHOLE = 61 * 1024 * 1024
F32, BF16 = jnp.float32, jnp.bfloat16


def hop(value, axis, steps):
    count = lax.axis_size(axis)
    return lax.ppermute(value, axis, [(s, (s + steps) % count) for s in range(count)])


def nn(a, b):
    return jnp.dot(a, b, preferred_element_type=F32)


def nt(a, b):
    return lax.dot_general(a, b, (((1,), (1,)), ((), ())), preferred_element_type=F32)


def tn(a, b):
    return lax.dot_general(a, b, (((0,), (0,)), ((), ())), preferred_element_type=F32)


def pick_rows(chosen, cands):
    spots = lax.broadcasted_iota(jnp.int32, (cands.shape[0], chosen.shape[1]), 0)
    return tn((spots == chosen).astype(BF16), cands)


def text_kernel(chosen_hbm, cand_hbm, weight_hbm, unit_ref, norm_ref, padded_ref, chosen_ref, cand_ref, weight_ref, wide_ref, sem):
    loads = [pltpu.make_async_copy(source, target, sem.at[k]) for k, (source, target) in enumerate(
        ((chosen_hbm, chosen_ref), (cand_hbm, cand_ref), (weight_hbm, weight_ref)))]
    for load in loads:
        load.start()
    wide_ref[...] = jnp.zeros_like(wide_ref)
    for load in loads:
        load.wait()
    texts = pick_rows(chosen_ref[...], cand_ref[...])
    norm = jnp.sqrt(jnp.sum(texts * texts, axis=1, keepdims=True) + EPS)
    unit_ref[...] = (texts / norm).astype(BF16)
    norm_ref[...] = norm
    wide_ref[:weight_ref.shape[0], :] = weight_ref[...].astype(F32)
    padded_ref[...] = wide_ref[...].astype(BF16)


def image_kernel(chosen_ref, cand_ref, out_ref):
    out_ref[...] = pick_rows(chosen_ref[...], cand_ref[...]).astype(BF16)


def pair_kernel(size, spot_ref, mine_ref, there_ref, deep_mine_ref, deep_other_ref, cols_mine_ref, cols_other_ref,
                flat_ref, group_ref, deep_ref):
    pairs, depth = mine_ref.shape
    first = spot_ref[0] == 0
    mine, there = mine_ref[...].astype(F32).T, there_ref[...].astype(F32).T
    flat_ref[:, :pairs] = jnp.where(first, mine, there)
    flat_ref[:, pairs:] = jnp.where(first, there, mine)
    deep_ref[...] = jnp.zeros_like(deep_ref)
    for block in range(depth // size):
        core, place = block % 2, block // 2
        rows = flat_ref[block * size:(block + 1) * size, :]
        group_ref[core, place * size:(place + 1) * size, :] = rows
        deep_ref[core, place * PADDED:place * PADDED + size, :] = rows
    core = spot_ref[2]
    cols_mine_ref[...] = group_ref[core].astype(BF16)
    cols_other_ref[...] = group_ref[1 - core].astype(BF16)
    deep_mine_ref[...] = deep_ref[core].T.astype(BF16)
    deep_other_ref[...] = deep_ref[1 - core].T.astype(BF16)


def half_kernel(deep_ref, weight_ref, out_ref):
    out_ref[...] = nn(deep_ref[...], weight_ref[...])


def unit_kernel(half_ref, deep_ref, weight_ref, unit_ref, norm_ref):
    proj = half_ref[...] + nn(deep_ref[...], weight_ref[...])
    norm = jnp.sqrt(jnp.sum(proj * proj, axis=1, keepdims=True) + EPS)
    unit_ref[...] = (proj / norm).astype(BF16)
    norm_ref[...] = norm


def main_kernel(scal_ref, spot_ref, unit_ref, norm_ref, cols_ref, text_ref, send_ref, back_ref, part_hbm,
                grad_ref, part_ref, sem):
    temper, offset, factor = scal_ref[0], scal_ref[1], scal_ref[2]
    unit = unit_ref[...]
    rows = unit.shape[0]
    pair = rows // 2
    row_id = lax.broadcasted_iota(jnp.int32, (rows, CHUNK), 0) - spot_ref[0]
    col_id = lax.broadcasted_iota(jnp.int32, (rows, CHUNK), 1) - spot_ref[1]
    inside = (row_id >= 0) & (row_id < pair)
    stores = []
    for k in range(text_ref.shape[0] // CHUNK):
        block = pl.ds(k * CHUNK, CHUNK)
        logits = temper * nt(unit, text_ref[block, :]) + offset
        sign = jnp.where(inside & (col_id + k * CHUNK == row_id), 1.0, -1.0)
        grad = (-factor * sign / (1.0 + jnp.exp(sign * logits))).astype(BF16)
        grad_ref[:, block] = grad
        part_ref[block, :] = tn(grad, unit).astype(BF16)
        store = pltpu.make_async_copy(part_ref.at[block], part_hbm.at[block], sem.at[k])
        store.start()
        stores.append(store)
    image_back = temper * nn(grad_ref[...], text_ref[...])
    unit_float = unit.astype(F32)
    radial = jnp.sum(unit_float * image_back, axis=1, keepdims=True)
    back = ((image_back - unit_float * radial) / norm_ref[...]).astype(BF16)
    back_ref[...] = back
    send_ref[...] = nn(cols_ref[...], back).astype(BF16)
    for store in stores:
        store.wait()


def fold_kernel(came_ref, out_ref, sum_ref, flat_ref):
    total = came_ref[0].astype(F32)
    for k in range(1, came_ref.shape[0]):
        total += came_ref[k].astype(F32)
    sum_ref[...] = total
    flat_ref[...] = jnp.zeros_like(flat_ref)
    pieces = flat_ref.shape[0]
    size = sum_ref.shape[0] // pieces
    for p in range(pieces):
        for t in range(sum_ref.shape[1] // LANES):
            flat_ref[p, t * size:(t + 1) * size, :] = sum_ref[p * size:(p + 1) * size, t * LANES:(t + 1) * LANES]
    out_ref[...] = flat_ref[...].astype(BF16)


def unfold_kernel(came_ref, out_ref, sum_ref):
    total = came_ref[0].astype(F32)
    for k in range(1, came_ref.shape[0]):
        total += came_ref[k].astype(F32)
    sum_ref[...] = total
    size = out_ref.shape[0]
    for t in range(out_ref.shape[1] // LANES):
        out_ref[:, t * LANES:(t + 1) * LANES] = sum_ref[t * size:(t + 1) * size, :]


def place_kernel(scal_ref, chosen_ref, back_ref, unit_ref, norm_ref, out_ref):
    back = scal_ref[0] * back_ref[...].astype(F32)
    unit = unit_ref[...].astype(F32)
    radial = jnp.sum(unit * back, axis=1, keepdims=True)
    rest = (back - unit * radial) / norm_ref[...]
    spots = lax.broadcasted_iota(jnp.int32, (out_ref.shape[0], rest.shape[0]), 0)
    here = (spots == chosen_ref[...]).astype(BF16)
    placed = None
    for _ in range(3):
        part = rest.astype(BF16)
        rest = rest - part.astype(F32)
        placed = nn(here, part) if placed is None else placed + nn(here, part)
    out_ref[...] = placed


def call(kernel, outs, in_specs, out_specs, scratch=(), cost=0, limit=LIMIT):
    return pl.pallas_call(
        kernel,
        out_shape=tuple(jax.ShapeDtypeStruct(shape, dtype) for shape, dtype in outs),
        in_specs=in_specs,
        out_specs=out_specs,
        scratch_shapes=list(scratch),
        compiler_params=pltpu.CompilerParams(vmem_limit_bytes=limit),
        cost_estimate=pl.CostEstimate(flops=cost, bytes_accessed=2_000_000, transcendentals=0),
    )


def shards(image_cand, text_cand, selection, head_weight, logit_temp, logit_offset, loss_scale):
    pairs = selection.shape[0]
    cands, depth = image_cand.shape
    own_rows, width = head_weight.shape
    rows = 2 * pairs
    n_y, n_x = lax.axis_size("y"), lax.axis_size("x")
    my_zl, my_y, core = (lax.axis_index(a) for a in ("zl", "y", "c"))
    total = pairs * lax.axis_size(ALL)
    spot = jnp.stack([my_zl * pairs, my_y * pairs, core])
    scalars = jnp.stack([logit_temp[0], logit_offset[0], loss_scale[0] / total])

    chosen = selection[None, :]
    text_unit, txt_norm, part = call(
        text_kernel, [((pairs, width), BF16), ((pairs, 1), F32), ((PADDED, width), BF16)], [HBM] * 3, (VMEM,) * 3,
        [pltpu.VMEM((1, pairs), jnp.int32), pltpu.VMEM((cands, depth), BF16), pltpu.VMEM((own_rows, width), BF16),
         pltpu.VMEM((PADDED, width), F32), pltpu.SemaphoreType.DMA((3,))],
        cost=2 * pairs * cands * width, limit=WHOLE,
    )(chosen, text_cand, head_weight)
    text_all = lax.all_gather(text_unit, "y", axis=0, tiled=True)

    slab = lax.all_gather(part, "zh", axis=0, tiled=True)
    slab, chosen = lax.optimization_barrier((slab, chosen))
    (picked,) = call(
        image_kernel, [((pairs, depth), BF16)], [VMEM, VMEM], (VMEM,), cost=2 * pairs * cands * depth,
    )(chosen, image_cand)
    there = hop(picked, "zl", 1)
    slabs = lax.all_to_all(jnp.broadcast_to(slab[None], (n_x,) + slab.shape), "x", 0, 0)
    mine = slabs.reshape(n_x * slab.shape[0], width)
    deep = mine.shape[0]
    deep_mine, deep_other, cols_mine, cols_other = call(
        lambda *refs: pair_kernel(own_rows, *refs),
        [((rows, deep), BF16), ((rows, deep), BF16), ((depth // 2, rows), BF16), ((depth // 2, rows), BF16)],
        [SMEM, VMEM, VMEM], (VMEM,) * 4,
        [pltpu.VMEM((depth, rows), F32), pltpu.VMEM((2, depth // 2, rows), F32), pltpu.VMEM((2, deep, rows), F32)],
    )(spot, picked, there)
    mine, deep_mine = lax.optimization_barrier((mine, deep_mine))
    other = hop(mine, "c", 1)
    (half,) = call(
        half_kernel, [((rows, width), F32)], [VMEM, VMEM], (VMEM,), cost=2 * rows * deep * width, limit=4 * 1024 * 1024,
    )(deep_mine, mine)
    image_unit, img_norm = call(
        unit_kernel, [((rows, width), BF16), ((rows, 1), F32)], [VMEM] * 3, (VMEM,) * 2, cost=2 * rows * deep * width,
    )(half, deep_other, other)
    send, proj_back, text_part = call(
        main_kernel,
        [((depth // 2, width), BF16), ((rows, width), BF16), ((n_y * pairs, width), BF16)],
        [SMEM, SMEM] + [VMEM] * 4, (VMEM, VMEM, HBM),
        [pltpu.VMEM((rows, n_y * pairs), BF16), pltpu.VMEM((n_y * pairs, width), BF16),
         pltpu.SemaphoreType.DMA((n_y * pairs // CHUNK,))],
        cost=6 * rows * n_y * pairs * width, limit=ROOMY,
    )(scalars, spot, image_unit, img_norm, cols_other, text_all)
    text_back = lax.psum_scatter(text_part.reshape(n_y, pairs, width), "y", scatter_dimension=0)
    got = hop(send, "c", 1)
    head = (nn(cols_mine, proj_back) + got.astype(F32)).astype(BF16)

    share = depth // 2 // n_x
    came = lax.all_to_all(head.reshape(n_x, share, width), "x", 0, 0)
    n_z = lax.axis_size(("zh", "zl"))
    piece = share // n_z
    strips = piece * (width // LANES)
    strips += -strips % 8
    (folded,) = call(
        fold_kernel, [((n_z, strips, LANES), BF16)], [VMEM], (VMEM,),
        [pltpu.VMEM((share, width), F32), pltpu.VMEM((n_z, strips, LANES), F32)],
    )(came)
    came = lax.all_to_all(folded, ("zh", "zl"), 0, 0)
    head = jnp.sum(came.astype(F32), axis=0).astype(BF16)
    came = lax.all_to_all(jnp.broadcast_to(head[None], (n_y,) + head.shape), "y", 0, 0)
    (head,) = call(unfold_kernel, [((piece, width), F32)], [VMEM], (VMEM,), [pltpu.VMEM((strips, LANES), F32)])(came)

    there = hop(head, "zl", 1)
    (text_grad,) = call(
        place_kernel, [((cands, width), F32)], [SMEM] + [VMEM] * 4, (VMEM,), cost=6 * cands * pairs * width,
    )(scalars, chosen, text_back, text_unit, txt_norm)
    there, text_grad = lax.optimization_barrier((there, text_grad))
    head_grad = jnp.concatenate([jnp.where(my_zl == 0, head, there), jnp.where(my_zl == 0, there, head)], axis=0)
    return head_grad, text_grad


def solution(mesh):
    devices = mesh.devices
    fine = Mesh(devices.reshape(2, devices.shape[0] // 2, 4, devices.shape[1] // 8, 2), ALL)
    return jax.shard_map(
        shards,
        mesh=fine,
        in_specs=(P(ALL, None), P(ALL, None), P(ALL), P(("x", "zh", "c"), None), P(), P(), P()),
        out_specs=(P(("x", "zh", "c"), None), P(ALL, None)),
        check_vma=False,
    )
```

```python
import jax
import jax.numpy as jnp
from jax import lax
from jax.experimental import pallas as pl
from jax.experimental.pallas import tpu as pltpu
from jax.sharding import Mesh, PartitionSpec as P

EPS = 1e-06
ALL = ("zl", "y", "x", "zh", "c")
PADDED = 40
CHUNK = 256
VMEM = pl.BlockSpec(memory_space=pltpu.VMEM)
SMEM = pl.BlockSpec(memory_space=pltpu.SMEM)
HBM = pl.BlockSpec(memory_space=pltpu.HBM)
LANES = 128
LIMIT = 8 * 1024 * 1024
ROOMY = 12 * 1024 * 1024
WHOLE = 61 * 1024 * 1024
F32, BF16 = jnp.float32, jnp.bfloat16


def hop(value, axis, steps):
    count = lax.axis_size(axis)
    return lax.ppermute(value, axis, [(s, (s + steps) % count) for s in range(count)])


def nn(a, b):
    return jnp.dot(a, b, preferred_element_type=F32)


def nt(a, b):
    return lax.dot_general(a, b, (((1,), (1,)), ((), ())), preferred_element_type=F32)


def tn(a, b):
    return lax.dot_general(a, b, (((0,), (0,)), ((), ())), preferred_element_type=F32)


def pick_rows(chosen, cands):
    spots = lax.broadcasted_iota(jnp.int32, (cands.shape[0], chosen.shape[1]), 0)
    return tn((spots == chosen).astype(BF16), cands)


def text_kernel(chosen_hbm, cand_hbm, weight_hbm, unit_ref, norm_ref, padded_ref, chosen_ref, cand_ref, weight_ref, wide_ref, sem):
    loads = [pltpu.make_async_copy(source, target, sem.at[k]) for k, (source, target) in enumerate(
        ((chosen_hbm, chosen_ref), (cand_hbm, cand_ref), (weight_hbm, weight_ref)))]
    for load in loads:
        load.start()
    wide_ref[...] = jnp.zeros_like(wide_ref)
    for load in loads:
        load.wait()
    texts = pick_rows(chosen_ref[...], cand_ref[...])
    norm = jnp.sqrt(jnp.sum(texts * texts, axis=1, keepdims=True) + EPS)
    unit_ref[...] = (texts / norm).astype(BF16)
    norm_ref[...] = norm
    wide_ref[:weight_ref.shape[0], :] = weight_ref[...].astype(F32)
    padded_ref[...] = wide_ref[...].astype(BF16)


def image_kernel(chosen_ref, cand_ref, out_ref):
    out_ref[...] = pick_rows(chosen_ref[...], cand_ref[...]).astype(BF16)


def pair_kernel(size, spot_ref, mine_ref, there_ref, deep_mine_ref, deep_other_ref, cols_mine_ref, cols_other_ref,
                flat_ref, group_ref, deep_ref):
    pairs, depth = mine_ref.shape
    first = spot_ref[0] == 0
    mine, there = mine_ref[...].astype(F32).T, there_ref[...].astype(F32).T
    flat_ref[:, :pairs] = jnp.where(first, mine, there)
    flat_ref[:, pairs:] = jnp.where(first, there, mine)
    deep_ref[...] = jnp.zeros_like(deep_ref)
    for block in range(depth // size):
        core, place = block % 2, block // 2
        rows = flat_ref[block * size:(block + 1) * size, :]
        group_ref[core, place * size:(place + 1) * size, :] = rows
        deep_ref[core, place * PADDED:place * PADDED + size, :] = rows
    core = spot_ref[2]
    cols_mine_ref[...] = group_ref[core].astype(BF16)
    cols_other_ref[...] = group_ref[1 - core].astype(BF16)
    deep_mine_ref[...] = deep_ref[core].T.astype(BF16)
    deep_other_ref[...] = deep_ref[1 - core].T.astype(BF16)


def half_kernel(deep_ref, weight_ref, out_ref):
    out_ref[...] = nn(deep_ref[...], weight_ref[...])


def unit_kernel(half_ref, deep_ref, weight_ref, unit_ref, norm_ref):
    proj = half_ref[...] + nn(deep_ref[...], weight_ref[...])
    norm = jnp.sqrt(jnp.sum(proj * proj, axis=1, keepdims=True) + EPS)
    unit_ref[...] = (proj / norm).astype(BF16)
    norm_ref[...] = norm


def main_kernel(scal_ref, spot_ref, unit_ref, norm_ref, text_ref, back_ref, part_hbm,
                grad_ref, part_ref, sem):
    temper, offset, factor = scal_ref[0], scal_ref[1], scal_ref[2]
    unit = unit_ref[...]
    rows = unit.shape[0]
    pair = rows // 2
    row_id = lax.broadcasted_iota(jnp.int32, (rows, CHUNK), 0) - spot_ref[0]
    col_id = lax.broadcasted_iota(jnp.int32, (rows, CHUNK), 1) - spot_ref[1]
    inside = (row_id >= 0) & (row_id < pair)
    stores = []
    for k in range(text_ref.shape[0] // CHUNK):
        block = pl.ds(k * CHUNK, CHUNK)
        logits = temper * nt(unit, text_ref[block, :]) + offset
        same = inside & (col_id + k * CHUNK == row_id)
        weight = jnp.where(same, -factor, factor)
        grad = (weight / (1.0 + jnp.exp(jnp.where(same, logits, -logits)))).astype(BF16)
        grad_ref[:, block] = grad
        part_ref[block, :] = tn(grad, unit).astype(BF16)
        store = pltpu.make_async_copy(part_ref.at[block], part_hbm.at[block], sem.at[k])
        store.start()
        stores.append(store)
    image_back = nn(grad_ref[...], text_ref[...])
    unit_float = unit.astype(F32)
    radial = jnp.sum(unit_float * image_back, axis=1, keepdims=True)
    back = ((image_back - unit_float * radial) * (temper / norm_ref[...])).astype(BF16)
    back_ref[...] = back
    for store in stores:
        store.wait()


def join_kernel(cols_mine_ref, cols_there_ref, back_ref, there_ref, out_ref):
    out_ref[...] = (nn(cols_mine_ref[...], back_ref[...]) + nn(cols_there_ref[...], there_ref[...])).astype(BF16)


def fold_kernel(came_ref, out_ref, sum_ref, flat_ref):
    total = came_ref[0].astype(F32)
    for k in range(1, came_ref.shape[0]):
        total += came_ref[k].astype(F32)
    sum_ref[...] = total
    flat_ref[...] = jnp.zeros_like(flat_ref)
    pieces = flat_ref.shape[0]
    size = sum_ref.shape[0] // pieces
    for p in range(pieces):
        for t in range(sum_ref.shape[1] // LANES):
            flat_ref[p, t * size:(t + 1) * size, :] = sum_ref[p * size:(p + 1) * size, t * LANES:(t + 1) * LANES]
    out_ref[...] = flat_ref[...].astype(BF16)


def unfold_kernel(came_ref, out_ref, sum_ref):
    total = came_ref[0].astype(F32)
    for k in range(1, came_ref.shape[0]):
        total += came_ref[k].astype(F32)
    sum_ref[...] = total
    size = out_ref.shape[0]
    for t in range(out_ref.shape[1] // LANES):
        out_ref[:, t * LANES:(t + 1) * LANES] = sum_ref[t * size:(t + 1) * size, :]


def place_kernel(scal_ref, chosen_ref, back_ref, unit_ref, norm_ref, out_ref):
    back = scal_ref[0] * back_ref[...].astype(F32)
    unit = unit_ref[...].astype(F32)
    radial = jnp.sum(unit * back, axis=1, keepdims=True)
    rest = (back - unit * radial) / norm_ref[...]
    spots = lax.broadcasted_iota(jnp.int32, (out_ref.shape[0], rest.shape[0]), 0)
    here = (spots == chosen_ref[...]).astype(BF16)
    placed = None
    for _ in range(3):
        part = rest.astype(BF16)
        rest = rest - part.astype(F32)
        placed = nn(here, part) if placed is None else placed + nn(here, part)
    out_ref[...] = placed


def call(kernel, outs, in_specs, out_specs, scratch=(), cost=0, limit=LIMIT):
    return pl.pallas_call(
        kernel,
        out_shape=tuple(jax.ShapeDtypeStruct(shape, dtype) for shape, dtype in outs),
        in_specs=in_specs,
        out_specs=out_specs,
        scratch_shapes=list(scratch),
        compiler_params=pltpu.CompilerParams(vmem_limit_bytes=limit),
        cost_estimate=pl.CostEstimate(flops=cost, bytes_accessed=2_000_000, transcendentals=0),
    )


def shards(image_cand, text_cand, selection, head_weight, logit_temp, logit_offset, loss_scale):
    pairs = selection.shape[0]
    cands, depth = image_cand.shape
    own_rows, width = head_weight.shape
    rows = 2 * pairs
    n_y, n_x = lax.axis_size("y"), lax.axis_size("x")
    my_zl, my_y, core = (lax.axis_index(a) for a in ("zl", "y", "c"))
    total = pairs * lax.axis_size(ALL)
    spot = jnp.stack([my_zl * pairs, my_y * pairs, core])
    scalars = jnp.stack([logit_temp[0], logit_offset[0], loss_scale[0] / total])

    chosen = selection[None, :]
    text_unit, txt_norm, part = call(
        text_kernel, [((pairs, width), BF16), ((pairs, 1), F32), ((PADDED, width), BF16)], [HBM] * 3, (VMEM,) * 3,
        [pltpu.VMEM((1, pairs), jnp.int32), pltpu.VMEM((cands, depth), BF16), pltpu.VMEM((own_rows, width), BF16),
         pltpu.VMEM((PADDED, width), F32), pltpu.SemaphoreType.DMA((3,))],
        cost=2 * pairs * cands * width, limit=WHOLE,
    )(chosen, text_cand, head_weight)
    text_all = lax.all_gather(text_unit, "y", axis=0, tiled=True)

    slab = lax.all_gather(part, "zh", axis=0, tiled=True)
    slab, chosen = lax.optimization_barrier((slab, chosen))
    (picked,) = call(
        image_kernel, [((pairs, depth), BF16)], [VMEM, VMEM], (VMEM,), cost=2 * pairs * cands * depth,
    )(chosen, image_cand)
    there = hop(picked, "zl", 1)
    slabs = lax.all_to_all(jnp.broadcast_to(slab[None], (n_x,) + slab.shape), "x", 0, 0)
    mine = slabs.reshape(n_x * slab.shape[0], width)
    deep = mine.shape[0]
    deep_mine, deep_other, cols_mine, cols_other = call(
        lambda *refs: pair_kernel(own_rows, *refs),
        [((rows, deep), BF16), ((rows, deep), BF16), ((depth // 2, rows), BF16), ((depth // 2, rows), BF16)],
        [SMEM, VMEM, VMEM], (VMEM,) * 4,
        [pltpu.VMEM((depth, rows), F32), pltpu.VMEM((2, depth // 2, rows), F32), pltpu.VMEM((2, deep, rows), F32)],
    )(spot, picked, there)
    cols_there = hop(cols_other, "c", 1)
    mine, cols_there = lax.optimization_barrier((mine, cols_there))
    other = hop(mine, "c", 1)
    (half,) = call(
        half_kernel, [((rows, width), F32)], [VMEM, VMEM], (VMEM,), cost=2 * rows * deep * width, limit=4 * 1024 * 1024,
    )(deep_mine, mine)
    image_unit, img_norm = call(
        unit_kernel, [((rows, width), BF16), ((rows, 1), F32)], [VMEM] * 3, (VMEM,) * 2, cost=2 * rows * deep * width,
    )(half, deep_other, other)
    proj_back, text_part = call(
        main_kernel,
        [((rows, width), BF16), ((n_y * pairs, width), BF16)],
        [SMEM, SMEM] + [VMEM] * 3, (VMEM, HBM),
        [pltpu.VMEM((rows, n_y * pairs), BF16), pltpu.VMEM((n_y * pairs, width), BF16),
         pltpu.SemaphoreType.DMA((n_y * pairs // CHUNK,))],
        cost=6 * rows * n_y * pairs * width, limit=ROOMY,
    )(scalars, spot, image_unit, img_norm, text_all)
    text_back = lax.psum_scatter(text_part.reshape(n_y, pairs, width), "y", scatter_dimension=0)
    (head,) = call(
        join_kernel, [((depth // 2, width), BF16)], [VMEM] * 4, (VMEM,), cost=2 * rows * depth * width,
    )(cols_mine, cols_there, proj_back, hop(proj_back, "c", 1))

    share = depth // 2 // n_x
    came = lax.all_to_all(head.reshape(n_x, share, width), "x", 0, 0)
    n_z = lax.axis_size(("zh", "zl"))
    piece = share // n_z
    strips = piece * (width // LANES)
    strips += -strips % 8
    (folded,) = call(
        fold_kernel, [((n_z, strips, LANES), BF16)], [VMEM], (VMEM,),
        [pltpu.VMEM((share, width), F32), pltpu.VMEM((n_z, strips, LANES), F32)],
    )(came)
    came = lax.all_to_all(folded, ("zh", "zl"), 0, 0)
    head = jnp.sum(came.astype(F32), axis=0).astype(BF16)
    came = lax.all_to_all(jnp.broadcast_to(head[None], (n_y,) + head.shape), "y", 0, 0)
    (head,) = call(unfold_kernel, [((piece, width), F32)], [VMEM], (VMEM,), [pltpu.VMEM((strips, LANES), F32)])(came)

    there = hop(head, "zl", 1)
    (text_grad,) = call(
        place_kernel, [((cands, width), F32)], [SMEM] + [VMEM] * 4, (VMEM,), cost=6 * cands * pairs * width,
    )(scalars, chosen, text_back, text_unit, txt_norm)
    there, text_grad = lax.optimization_barrier((there, text_grad))
    head_grad = jnp.concatenate([jnp.where(my_zl == 0, head, there), jnp.where(my_zl == 0, there, head)], axis=0)
    return head_grad, text_grad


def solution(mesh):
    devices = mesh.devices
    fine = Mesh(devices.reshape(2, devices.shape[0] // 2, 4, devices.shape[1] // 8, 2), ALL)
    return jax.shard_map(
        shards,
        mesh=fine,
        in_specs=(P(ALL, None), P(ALL, None), P(ALL), P(("x", "zh", "c"), None), P(), P(), P()),
        out_specs=(P(("x", "zh", "c"), None), P(ALL, None)),
        check_vma=False,
    )
```

```python
import jax
import jax.numpy as jnp
from jax import lax
from jax.experimental import pallas as pl
from jax.experimental.pallas import tpu as pltpu
from jax.sharding import Mesh, PartitionSpec as P

EPS = 1e-06
ALL = ("zl", "y", "x", "zh", "c")
PADDED = 40
CHUNK = 256
VMEM = pl.BlockSpec(memory_space=pltpu.VMEM)
SMEM = pl.BlockSpec(memory_space=pltpu.SMEM)
HBM = pl.BlockSpec(memory_space=pltpu.HBM)
LANES = 128
LIMIT = 8 * 1024 * 1024
ROOMY = 12 * 1024 * 1024
WHOLE = 61 * 1024 * 1024
F32, BF16 = jnp.float32, jnp.bfloat16


def hop(value, axis, steps):
    count = lax.axis_size(axis)
    return lax.ppermute(value, axis, [(s, (s + steps) % count) for s in range(count)])


def nn(a, b):
    return jnp.dot(a, b, preferred_element_type=F32)


def nt(a, b):
    return lax.dot_general(a, b, (((1,), (1,)), ((), ())), preferred_element_type=F32)


def tn(a, b):
    return lax.dot_general(a, b, (((0,), (0,)), ((), ())), preferred_element_type=F32)


def pick_rows(chosen, cands):
    spots = lax.broadcasted_iota(jnp.int32, (cands.shape[0], chosen.shape[1]), 0)
    return tn((spots == chosen).astype(BF16), cands)


def text_kernel(chosen_hbm, cand_hbm, weight_hbm, unit_ref, norm_ref, padded_ref, chosen_ref, cand_ref, weight_ref, wide_ref, sem):
    loads = [pltpu.make_async_copy(source, target, sem.at[k]) for k, (source, target) in enumerate(
        ((chosen_hbm, chosen_ref), (cand_hbm, cand_ref), (weight_hbm, weight_ref)))]
    for load in loads:
        load.start()
    wide_ref[...] = jnp.zeros_like(wide_ref)
    for load in loads:
        load.wait()
    texts = pick_rows(chosen_ref[...], cand_ref[...])
    norm = jnp.sqrt(jnp.sum(texts * texts, axis=1, keepdims=True) + EPS)
    unit_ref[...] = (texts / norm).astype(BF16)
    norm_ref[...] = norm
    wide_ref[:weight_ref.shape[0], :] = weight_ref[...].astype(F32)
    padded_ref[...] = wide_ref[...].astype(BF16)


def image_kernel(chosen_ref, cand_ref, out_ref):
    out_ref[...] = pick_rows(chosen_ref[...], cand_ref[...]).astype(BF16)


def pair_kernel(size, n_zh, spot_ref, mine_ref, there_ref, deep_mine_ref, deep_other_ref, cols_mine_ref, cols_other_ref,
                flat_ref, group_ref, deep_ref):
    pairs, depth = mine_ref.shape
    first = spot_ref[0] == 0
    mine, there = mine_ref[...].astype(F32).T, there_ref[...].astype(F32).T
    flat_ref[:, :pairs] = jnp.where(first, mine, there)
    flat_ref[:, pairs:] = jnp.where(first, there, mine)
    deep_ref[...] = jnp.zeros_like(deep_ref)
    for block in range(depth // size):
        core, place = block % 2, block // 2
        rows = flat_ref[block * size:(block + 1) * size, :]
        part = size // 2
        start = (place // n_zh * 2 * n_zh + place % n_zh) * part
        group_ref[core, start:start + part, :] = rows[:part]
        group_ref[core, start + n_zh * part:start + (n_zh + 1) * part, :] = rows[part:]
        deep_ref[core, place * PADDED:place * PADDED + size, :] = rows
    core = spot_ref[2]
    cols_mine_ref[...] = group_ref[core].astype(BF16)
    cols_other_ref[...] = group_ref[1 - core].astype(BF16)
    deep_mine_ref[...] = deep_ref[core].T.astype(BF16)
    deep_other_ref[...] = deep_ref[1 - core].T.astype(BF16)


def half_kernel(deep_ref, weight_ref, out_ref):
    out_ref[...] = nn(deep_ref[...], weight_ref[...])


def unit_kernel(half_ref, deep_ref, weight_ref, unit_ref, norm_ref):
    proj = half_ref[...] + nn(deep_ref[...], weight_ref[...])
    norm = jnp.sqrt(jnp.sum(proj * proj, axis=1, keepdims=True) + EPS)
    unit_ref[...] = (proj / norm).astype(BF16)
    norm_ref[...] = norm


def main_kernel(scal_ref, spot_ref, unit_ref, norm_ref, text_ref, back_ref, part_hbm,
                grad_ref, part_ref, sem):
    temper, offset, factor = scal_ref[0], scal_ref[1], scal_ref[2]
    unit = unit_ref[...]
    rows = unit.shape[0]
    pair = rows // 2
    row_id = lax.broadcasted_iota(jnp.int32, (rows, CHUNK), 0) - spot_ref[0]
    col_id = lax.broadcasted_iota(jnp.int32, (rows, CHUNK), 1) - spot_ref[1]
    inside = (row_id >= 0) & (row_id < pair)
    stores = []
    for k in range(text_ref.shape[0] // CHUNK):
        block = pl.ds(k * CHUNK, CHUNK)
        logits = temper * nt(unit, text_ref[block, :]) + offset
        same = inside & (col_id + k * CHUNK == row_id)
        weight = jnp.where(same, -factor, factor)
        grad = (weight / (1.0 + jnp.exp(jnp.where(same, logits, -logits)))).astype(BF16)
        grad_ref[:, block] = grad
        part_ref[block, :] = tn(grad, unit).astype(BF16)
        store = pltpu.make_async_copy(part_ref.at[block], part_hbm.at[block], sem.at[k])
        store.start()
        stores.append(store)
    image_back = nn(grad_ref[...], text_ref[...])
    unit_float = unit.astype(F32)
    radial = jnp.sum(unit_float * image_back, axis=1, keepdims=True)
    back = ((image_back - unit_float * radial) * (temper / norm_ref[...])).astype(BF16)
    back_ref[...] = back
    for store in stores:
        store.wait()


def join_kernel(cols_mine_ref, cols_there_ref, back_ref, there_ref, out_ref):
    out_ref[...] = (nn(cols_mine_ref[...], back_ref[...]) + nn(cols_there_ref[...], there_ref[...])).astype(BF16)


def fold_kernel(came_ref, out_ref, sum_ref, flat_ref):
    total = came_ref[0].astype(F32)
    for k in range(1, came_ref.shape[0]):
        total += came_ref[k].astype(F32)
    sum_ref[...] = total
    flat_ref[...] = jnp.zeros_like(flat_ref)
    pieces = flat_ref.shape[0]
    size = sum_ref.shape[0] // pieces
    for p in range(pieces):
        for t in range(sum_ref.shape[1] // LANES):
            flat_ref[p, t * size:(t + 1) * size, :] = sum_ref[p * size:(p + 1) * size, t * LANES:(t + 1) * LANES]
    out_ref[...] = flat_ref[...].astype(BF16)


def unfold_kernel(came_ref, out_ref, sum_ref):
    total = came_ref[0].astype(F32)
    for k in range(1, came_ref.shape[0]):
        total += came_ref[k].astype(F32)
    sum_ref[...] = total
    size = out_ref.shape[0]
    for t in range(out_ref.shape[1] // LANES):
        out_ref[:, t * LANES:(t + 1) * LANES] = sum_ref[t * size:(t + 1) * size, :]


def place_kernel(scal_ref, chosen_ref, back_ref, unit_ref, norm_ref, out_ref):
    back = scal_ref[0] * back_ref[...].astype(F32)
    unit = unit_ref[...].astype(F32)
    radial = jnp.sum(unit * back, axis=1, keepdims=True)
    rest = (back - unit * radial) / norm_ref[...]
    spots = lax.broadcasted_iota(jnp.int32, (out_ref.shape[0], rest.shape[0]), 0)
    here = (spots == chosen_ref[...]).astype(BF16)
    placed = None
    for _ in range(3):
        part = rest.astype(BF16)
        rest = rest - part.astype(F32)
        placed = nn(here, part) if placed is None else placed + nn(here, part)
    out_ref[...] = placed


def call(kernel, outs, in_specs, out_specs, scratch=(), cost=0, limit=LIMIT):
    return pl.pallas_call(
        kernel,
        out_shape=tuple(jax.ShapeDtypeStruct(shape, dtype) for shape, dtype in outs),
        in_specs=in_specs,
        out_specs=out_specs,
        scratch_shapes=list(scratch),
        compiler_params=pltpu.CompilerParams(vmem_limit_bytes=limit),
        cost_estimate=pl.CostEstimate(flops=cost, bytes_accessed=2_000_000, transcendentals=0),
    )


def shards(image_cand, text_cand, selection, head_weight, logit_temp, logit_offset, loss_scale):
    pairs = selection.shape[0]
    cands, depth = image_cand.shape
    own_rows, width = head_weight.shape
    rows = 2 * pairs
    n_y, n_x, n_zh = lax.axis_size("y"), lax.axis_size("x"), lax.axis_size("zh")
    my_zl, my_y, core = (lax.axis_index(a) for a in ("zl", "y", "c"))
    total = pairs * lax.axis_size(ALL)
    spot = jnp.stack([my_zl * pairs, my_y * pairs, core])
    scalars = jnp.stack([logit_temp[0], logit_offset[0], loss_scale[0] / total])

    chosen = selection[None, :]
    text_unit, txt_norm, part = call(
        text_kernel, [((pairs, width), BF16), ((pairs, 1), F32), ((PADDED, width), BF16)], [HBM] * 3, (VMEM,) * 3,
        [pltpu.VMEM((1, pairs), jnp.int32), pltpu.VMEM((cands, depth), BF16), pltpu.VMEM((own_rows, width), BF16),
         pltpu.VMEM((PADDED, width), F32), pltpu.SemaphoreType.DMA((3,))],
        cost=2 * pairs * cands * width, limit=WHOLE,
    )(chosen, text_cand, head_weight)
    text_all = lax.all_gather(text_unit, "y", axis=0, tiled=True)

    slab = lax.all_gather(part, "zh", axis=0, tiled=True)
    slab, chosen = lax.optimization_barrier((slab, chosen))
    (picked,) = call(
        image_kernel, [((pairs, depth), BF16)], [VMEM, VMEM], (VMEM,), cost=2 * pairs * cands * depth,
    )(chosen, image_cand)
    there = hop(picked, "zl", 1)
    slabs = lax.all_to_all(jnp.broadcast_to(slab[None], (n_x,) + slab.shape), "x", 0, 0)
    mine = slabs.reshape(n_x * slab.shape[0], width)
    deep = mine.shape[0]
    deep_mine, deep_other, cols_mine, cols_other = call(
        lambda *refs: pair_kernel(own_rows, n_zh, *refs),
        [((rows, deep), BF16), ((rows, deep), BF16), ((depth // 2, rows), BF16), ((depth // 2, rows), BF16)],
        [SMEM, VMEM, VMEM], (VMEM,) * 4,
        [pltpu.VMEM((depth, rows), F32), pltpu.VMEM((2, depth // 2, rows), F32), pltpu.VMEM((2, deep, rows), F32)],
    )(spot, picked, there)
    cols_there = hop(cols_other, "c", 1)
    mine, cols_there = lax.optimization_barrier((mine, cols_there))
    other = hop(mine, "c", 1)
    (half,) = call(
        half_kernel, [((rows, width), F32)], [VMEM, VMEM], (VMEM,), cost=2 * rows * deep * width, limit=4 * 1024 * 1024,
    )(deep_mine, mine)
    image_unit, img_norm = call(
        unit_kernel, [((rows, width), BF16), ((rows, 1), F32)], [VMEM] * 3, (VMEM,) * 2, cost=2 * rows * deep * width,
    )(half, deep_other, other)
    proj_back, text_part = call(
        main_kernel,
        [((rows, width), BF16), ((n_y * pairs, width), BF16)],
        [SMEM, SMEM] + [VMEM] * 3, (VMEM, HBM),
        [pltpu.VMEM((rows, n_y * pairs), BF16), pltpu.VMEM((n_y * pairs, width), BF16),
         pltpu.SemaphoreType.DMA((n_y * pairs // CHUNK,))],
        cost=6 * rows * n_y * pairs * width, limit=ROOMY,
    )(scalars, spot, image_unit, img_norm, text_all)
    text_back = lax.psum_scatter(text_part.reshape(n_y, pairs, width), "y", scatter_dimension=0)
    (head,) = call(
        join_kernel, [((depth // 2, width), BF16)], [VMEM] * 4, (VMEM,), cost=2 * rows * depth * width,
    )(cols_mine, cols_there, proj_back, hop(proj_back, "c", 1))

    share = depth // 4 // n_x
    came = lax.all_to_all(head.reshape(2 * n_x, share, width), ("x", "zl"), 0, 0)
    piece = share // n_zh
    strips = piece * (width // LANES)
    strips += -strips % 8
    (folded,) = call(
        fold_kernel, [((n_zh, strips, LANES), BF16)], [VMEM], (VMEM,),
        [pltpu.VMEM((share, width), F32), pltpu.VMEM((n_zh, strips, LANES), F32)],
    )(came)
    came = lax.all_to_all(folded, "zh", 0, 0)
    head = jnp.sum(came.astype(F32), axis=0).astype(BF16)
    came = lax.all_to_all(jnp.broadcast_to(head[None], (n_y,) + head.shape), "y", 0, 0)
    (head,) = call(unfold_kernel, [((piece, width), F32)], [VMEM], (VMEM,), [pltpu.VMEM((strips, LANES), F32)])(came)

    there = hop(head, "zl", 1)
    (text_grad,) = call(
        place_kernel, [((cands, width), F32)], [SMEM] + [VMEM] * 4, (VMEM,), cost=6 * cands * pairs * width,
    )(scalars, chosen, text_back, text_unit, txt_norm)
    there, text_grad = lax.optimization_barrier((there, text_grad))
    head_grad = jnp.concatenate([jnp.where(my_zl == 0, head, there), jnp.where(my_zl == 0, there, head)], axis=0)
    return head_grad, text_grad


def solution(mesh):
    devices = mesh.devices
    fine = Mesh(devices.reshape(2, devices.shape[0] // 2, 4, devices.shape[1] // 8, 2), ALL)
    return jax.shard_map(
        shards,
        mesh=fine,
        in_specs=(P(ALL, None), P(ALL, None), P(ALL), P(("x", "zh", "c"), None), P(), P(), P()),
        out_specs=(P(("x", "zh", "c"), None), P(ALL, None)),
        check_vma=False,
    )
```

```python
import jax
import jax.numpy as jnp
from jax import lax
from jax.experimental import pallas as pl
from jax.experimental.pallas import tpu as pltpu
from jax.sharding import Mesh, PartitionSpec as P

EPS = 1e-06
ALL = ("zl", "y", "x", "zh", "c")
PADDED = 40
CHUNK = 256
VMEM = pl.BlockSpec(memory_space=pltpu.VMEM)
SMEM = pl.BlockSpec(memory_space=pltpu.SMEM)
HBM = pl.BlockSpec(memory_space=pltpu.HBM)
LANES = 128
LIMIT = 8 * 1024 * 1024
ROOMY = 12 * 1024 * 1024
WHOLE = 61 * 1024 * 1024
F32, BF16 = jnp.float32, jnp.bfloat16


def hop(value, axis, steps):
    count = lax.axis_size(axis)
    return lax.ppermute(value, axis, [(s, (s + steps) % count) for s in range(count)])


def nn(a, b):
    return jnp.dot(a, b, preferred_element_type=F32)


def nt(a, b):
    return lax.dot_general(a, b, (((1,), (1,)), ((), ())), preferred_element_type=F32)


def tn(a, b):
    return lax.dot_general(a, b, (((0,), (0,)), ((), ())), preferred_element_type=F32)


def pick_rows(chosen, cands):
    spots = lax.broadcasted_iota(jnp.int32, (cands.shape[0], chosen.shape[1]), 0)
    return tn((spots == chosen).astype(BF16), cands)


def text_kernel(chosen_hbm, cand_hbm, unit_ref, norm_ref, chosen_ref, cand_ref, sem):
    loads = [pltpu.make_async_copy(source, target, sem.at[k]) for k, (source, target) in enumerate(
        ((chosen_hbm, chosen_ref), (cand_hbm, cand_ref)))]
    for load in loads:
        load.start()
    for load in loads:
        load.wait()
    texts = pick_rows(chosen_ref[...], cand_ref[...])
    norm = jnp.sqrt(jnp.sum(texts * texts, axis=1, keepdims=True) + EPS)
    unit_ref[...] = (texts / norm).astype(BF16)
    norm_ref[...] = norm


def image_kernel(chosen_ref, cand_ref, out_ref):
    out_ref[...] = pick_rows(chosen_ref[...], cand_ref[...]).astype(BF16)


def pair_kernel(size, n_zh, spot_ref, mine_ref, there_ref, deep_mine_ref, deep_other_ref, cols_mine_ref, cols_other_ref,
                flat_ref, group_ref, deep_ref):
    pairs, depth = mine_ref.shape
    first = spot_ref[0] == 0
    mine, there = mine_ref[...].astype(F32).T, there_ref[...].astype(F32).T
    flat_ref[:, :pairs] = jnp.where(first, mine, there)
    flat_ref[:, pairs:] = jnp.where(first, there, mine)
    deep_ref[...] = jnp.zeros_like(deep_ref)
    for block in range(depth // size):
        core, place = block % 2, block // 2
        rows = flat_ref[block * size:(block + 1) * size, :]
        part = size // 2
        start = (place // n_zh * 2 * n_zh + place % n_zh) * part
        group_ref[core, start:start + part, :] = rows[:part]
        group_ref[core, start + n_zh * part:start + (n_zh + 1) * part, :] = rows[part:]
        deep_ref[core, place * PADDED:place * PADDED + size, :] = rows
    core = spot_ref[2]
    cols_mine_ref[...] = group_ref[core].astype(BF16)
    cols_other_ref[...] = group_ref[1 - core].astype(BF16)
    deep_mine_ref[...] = deep_ref[core].T.astype(BF16)
    deep_other_ref[...] = deep_ref[1 - core].T.astype(BF16)


def half_kernel(deep_ref, weight_ref, out_ref):
    out_ref[...] = nn(deep_ref[...], weight_ref[...])


def unit_kernel(half_ref, deep_ref, weight_ref, unit_ref, norm_ref):
    proj = half_ref[...] + nn(deep_ref[...], weight_ref[...])
    norm = jnp.sqrt(jnp.sum(proj * proj, axis=1, keepdims=True) + EPS)
    unit_ref[...] = (proj / norm).astype(BF16)
    norm_ref[...] = norm


def main_kernel(scal_ref, spot_ref, unit_ref, norm_ref, text_ref, back_ref, part_hbm,
                grad_ref, part_ref, sem):
    temper, offset, factor = scal_ref[0], scal_ref[1], scal_ref[2]
    unit = unit_ref[...]
    rows = unit.shape[0]
    pair = rows // 2
    row_id = lax.broadcasted_iota(jnp.int32, (rows, CHUNK), 0) - spot_ref[0]
    col_id = lax.broadcasted_iota(jnp.int32, (rows, CHUNK), 1) - spot_ref[1]
    inside = (row_id >= 0) & (row_id < pair)
    stores = []
    for k in range(text_ref.shape[0] // CHUNK):
        block = pl.ds(k * CHUNK, CHUNK)
        logits = temper * nt(unit, text_ref[block, :]) + offset
        same = inside & (col_id + k * CHUNK == row_id)
        weight = jnp.where(same, -factor, factor)
        grad = (weight / (1.0 + jnp.exp(jnp.where(same, logits, -logits)))).astype(BF16)
        grad_ref[:, block] = grad
        part_ref[block, :] = tn(grad, unit).astype(BF16)
        store = pltpu.make_async_copy(part_ref.at[block], part_hbm.at[block], sem.at[k])
        store.start()
        stores.append(store)
    image_back = nn(grad_ref[...], text_ref[...])
    unit_float = unit.astype(F32)
    radial = jnp.sum(unit_float * image_back, axis=1, keepdims=True)
    back = ((image_back - unit_float * radial) * (temper / norm_ref[...])).astype(BF16)
    back_ref[...] = back
    for store in stores:
        store.wait()


def join_kernel(own_ref, cols_ref, back_ref, out_ref):
    out_ref[...] = (own_ref[...] + nn(cols_ref[...], back_ref[...])).astype(BF16)


def fold_kernel(came_ref, out_ref, sum_ref, flat_ref):
    share = sum_ref.shape[0]
    total = None
    for k in range(came_ref.shape[0]):
        both = came_ref[k].astype(F32)
        both = both[:share] + both[share:]
        total = both if total is None else total + both
    sum_ref[...] = total
    flat_ref[...] = jnp.zeros_like(flat_ref)
    pieces = flat_ref.shape[0]
    size = sum_ref.shape[0] // pieces
    for p in range(pieces):
        for t in range(sum_ref.shape[1] // LANES):
            flat_ref[p, t * size:(t + 1) * size, :] = sum_ref[p * size:(p + 1) * size, t * LANES:(t + 1) * LANES]
    out_ref[...] = flat_ref[...].astype(BF16)


def unfold_kernel(came_ref, out_ref, sum_ref):
    total = came_ref[0].astype(F32)
    for k in range(1, came_ref.shape[0]):
        total += came_ref[k].astype(F32)
    sum_ref[...] = total
    size = out_ref.shape[0]
    for t in range(out_ref.shape[1] // LANES):
        out_ref[:, t * LANES:(t + 1) * LANES] = sum_ref[t * size:(t + 1) * size, :]


def place_kernel(scal_ref, chosen_ref, back_ref, unit_ref, norm_ref, out_ref):
    back = scal_ref[0] * back_ref[...].astype(F32)
    unit = unit_ref[...].astype(F32)
    radial = jnp.sum(unit * back, axis=1, keepdims=True)
    rest = (back - unit * radial) / norm_ref[...]
    spots = lax.broadcasted_iota(jnp.int32, (out_ref.shape[0], rest.shape[0]), 0)
    here = (spots == chosen_ref[...]).astype(BF16)
    placed = None
    for _ in range(3):
        part = rest.astype(BF16)
        rest = rest - part.astype(F32)
        placed = nn(here, part) if placed is None else placed + nn(here, part)
    out_ref[...] = placed


def call(kernel, outs, in_specs, out_specs, scratch=(), cost=0, limit=LIMIT):
    return pl.pallas_call(
        kernel,
        out_shape=tuple(jax.ShapeDtypeStruct(shape, dtype) for shape, dtype in outs),
        in_specs=in_specs,
        out_specs=out_specs,
        scratch_shapes=list(scratch),
        compiler_params=pltpu.CompilerParams(vmem_limit_bytes=limit),
        cost_estimate=pl.CostEstimate(flops=cost, bytes_accessed=2_000_000, transcendentals=0),
    )


def shards(image_cand, text_cand, selection, head_weight, logit_temp, logit_offset, loss_scale):
    pairs = selection.shape[0]
    cands, depth = image_cand.shape
    own_rows, width = head_weight.shape
    rows = 2 * pairs
    n_y, n_x, n_zh = lax.axis_size("y"), lax.axis_size("x"), lax.axis_size("zh")
    my_zl, my_y, core = (lax.axis_index(a) for a in ("zl", "y", "c"))
    total = pairs * lax.axis_size(ALL)
    spot = jnp.stack([my_zl * pairs, my_y * pairs, core])
    scalars = jnp.stack([logit_temp[0], logit_offset[0], loss_scale[0] / total])

    chosen = selection[None, :]
    text_unit, txt_norm = call(
        text_kernel, [((pairs, width), BF16), ((pairs, 1), F32)], [HBM] * 2, (VMEM,) * 2,
        [pltpu.VMEM((1, pairs), jnp.int32), pltpu.VMEM((cands, depth), BF16), pltpu.SemaphoreType.DMA((2,))],
        cost=2 * pairs * cands * width, limit=WHOLE,
    )(chosen, text_cand)
    text_all = lax.all_gather(text_unit, "y", axis=0, tiled=True)

    part = jnp.pad(head_weight, ((0, PADDED - own_rows), (0, 0)))
    slab = lax.all_gather(part, "zh", axis=0, tiled=True)
    slab, chosen = lax.optimization_barrier((slab, chosen))
    (picked,) = call(
        image_kernel, [((pairs, depth), BF16)], [VMEM, VMEM], (VMEM,), cost=2 * pairs * cands * depth,
    )(chosen, image_cand)
    there = hop(picked, "zl", 1)
    slabs = lax.all_to_all(jnp.broadcast_to(slab[None], (n_x,) + slab.shape), "x", 0, 0)
    mine = slabs.reshape(n_x * slab.shape[0], width)
    deep = mine.shape[0]
    deep_mine, deep_other, cols_mine, cols_other = call(
        lambda *refs: pair_kernel(own_rows, n_zh, *refs),
        [((rows, deep), BF16), ((rows, deep), BF16), ((depth // 2, rows), BF16), ((depth // 2, rows), BF16)],
        [SMEM, VMEM, VMEM], (VMEM,) * 4,
        [pltpu.VMEM((depth, rows), F32), pltpu.VMEM((2, depth // 2, rows), F32), pltpu.VMEM((2, deep, rows), F32)],
    )(spot, picked, there)
    cols_there = hop(cols_other, "c", 1)
    mine, cols_there = lax.optimization_barrier((mine, cols_there))
    other = hop(mine, "c", 1)
    (half,) = call(
        half_kernel, [((rows, width), F32)], [VMEM, VMEM], (VMEM,), cost=2 * rows * deep * width, limit=4 * 1024 * 1024,
    )(deep_mine, mine)
    image_unit, img_norm = call(
        unit_kernel, [((rows, width), BF16), ((rows, 1), F32)], [VMEM] * 3, (VMEM,) * 2, cost=2 * rows * deep * width,
    )(half, deep_other, other)
    proj_back, text_part = call(
        main_kernel,
        [((rows, width), BF16), ((n_y * pairs, width), BF16)],
        [SMEM, SMEM] + [VMEM] * 3, (VMEM, HBM),
        [pltpu.VMEM((rows, n_y * pairs), BF16), pltpu.VMEM((n_y * pairs, width), BF16),
         pltpu.SemaphoreType.DMA((n_y * pairs // CHUNK,))],
        cost=6 * rows * n_y * pairs * width, limit=ROOMY,
    )(scalars, spot, image_unit, img_norm, text_all)
    text_back = lax.psum_scatter(text_part.reshape(n_y, pairs, width), "y", scatter_dimension=0)
    back_there = hop(proj_back, "c", 1)
    (own,) = call(
        half_kernel, [((depth // 2, width), F32)], [VMEM] * 2, (VMEM,), cost=rows * depth * width,
    )(cols_mine, proj_back)
    (head,) = call(
        join_kernel, [((depth // 2, width), BF16)], [VMEM] * 3, (VMEM,), cost=rows * depth * width,
    )(own, cols_there, back_there)

    share = depth // 4 // n_x
    came = lax.all_to_all(head.reshape(2 * n_x, share, width), ("x", "zl"), 0, 0)
    piece = share // n_zh
    strips = piece * (width // LANES)
    strips += -strips % 16
    (folded,) = call(
        fold_kernel, [((n_zh, strips, LANES), BF16)], [VMEM], (VMEM,),
        [pltpu.VMEM((share, width), F32), pltpu.VMEM((n_zh, strips, LANES), F32)],
    )(came.reshape(n_x, 2 * share, width))
    came = lax.all_to_all(folded, "zh", 0, 0)
    head = jnp.sum(came.astype(F32), axis=0).astype(BF16)
    came = lax.all_to_all(jnp.broadcast_to(head[None], (n_y,) + head.shape), "y", 0, 0)
    (head,) = call(unfold_kernel, [((piece, width), F32)], [VMEM], (VMEM,), [pltpu.VMEM((strips, LANES), F32)])(came)

    there = hop(head, "zl", 1)
    (text_grad,) = call(
        place_kernel, [((cands, width), F32)], [SMEM] + [VMEM] * 4, (VMEM,), cost=6 * cands * pairs * width,
    )(scalars, chosen, text_back, text_unit, txt_norm)
    there, text_grad = lax.optimization_barrier((there, text_grad))
    head_grad = jnp.concatenate([jnp.where(my_zl == 0, head, there), jnp.where(my_zl == 0, there, head)], axis=0)
    return head_grad, text_grad


def solution(mesh):
    devices = mesh.devices
    fine = Mesh(devices.reshape(2, devices.shape[0] // 2, 4, devices.shape[1] // 8, 2), ALL)
    return jax.shard_map(
        shards,
        mesh=fine,
        in_specs=(P(ALL, None), P(ALL, None), P(ALL), P(("x", "zh", "c"), None), P(), P(), P()),
        out_specs=(P(("x", "zh", "c"), None), P(ALL, None)),
        check_vma=False,
    )
```

```python
import jax
import jax.numpy as jnp
from jax import lax
from jax.experimental import pallas as pl
from jax.experimental.pallas import tpu as pltpu
from jax.sharding import Mesh, PartitionSpec as P

EPS = 1e-06
ALL = ("zl", "y", "x", "zh", "c")
PADDED = 40
CHUNK = 512
VMEM = pl.BlockSpec(memory_space=pltpu.VMEM)
SMEM = pl.BlockSpec(memory_space=pltpu.SMEM)
HBM = pl.BlockSpec(memory_space=pltpu.HBM)
LANES = 128
LIMIT = 8 * 1024 * 1024
ROOMY = 12 * 1024 * 1024
WHOLE = 61 * 1024 * 1024
F32, BF16 = jnp.float32, jnp.bfloat16


def hop(value, axis, steps):
    count = lax.axis_size(axis)
    return lax.ppermute(value, axis, [(s, (s + steps) % count) for s in range(count)])


def nn(a, b):
    return jnp.dot(a, b, preferred_element_type=F32)


def nt(a, b):
    return lax.dot_general(a, b, (((1,), (1,)), ((), ())), preferred_element_type=F32)


def tn(a, b):
    return lax.dot_general(a, b, (((0,), (0,)), ((), ())), preferred_element_type=F32)


def pick_rows(chosen, cands):
    spots = lax.broadcasted_iota(jnp.int32, (cands.shape[0], chosen.shape[1]), 0)
    return tn((spots == chosen).astype(BF16), cands)


def text_kernel(chosen_hbm, cand_hbm, unit_ref, norm_ref, chosen_ref, cand_ref, sem):
    loads = [pltpu.make_async_copy(source, target, sem.at[k]) for k, (source, target) in enumerate(
        ((chosen_hbm, chosen_ref), (cand_hbm, cand_ref)))]
    for load in loads:
        load.start()
    for load in loads:
        load.wait()
    texts = pick_rows(chosen_ref[...], cand_ref[...])
    norm = jnp.sqrt(jnp.sum(texts * texts, axis=1, keepdims=True) + EPS)
    unit_ref[...] = (texts / norm).astype(BF16)
    norm_ref[...] = norm


def image_kernel(chosen_ref, cand_ref, out_ref):
    out_ref[...] = pick_rows(chosen_ref[...], cand_ref[...]).astype(BF16)


def pair_kernel(size, n_zh, spot_ref, mine_ref, there_ref, deep_mine_ref, deep_other_ref, cols_mine_ref, cols_other_ref,
                flat_ref, group_ref, deep_ref):
    pairs, depth = mine_ref.shape
    first = spot_ref[0] == 0
    mine, there = mine_ref[...].astype(F32).T, there_ref[...].astype(F32).T
    flat_ref[:, :pairs] = jnp.where(first, mine, there)
    flat_ref[:, pairs:] = jnp.where(first, there, mine)
    deep_ref[...] = jnp.zeros_like(deep_ref)
    for block in range(depth // size):
        core, place = block % 2, block // 2
        rows = flat_ref[block * size:(block + 1) * size, :]
        part = size // 2
        start = (place // n_zh * 2 * n_zh + place % n_zh) * part
        group_ref[core, start:start + part, :] = rows[:part]
        group_ref[core, start + n_zh * part:start + (n_zh + 1) * part, :] = rows[part:]
        deep_ref[core, place * PADDED:place * PADDED + size, :] = rows
    core = spot_ref[2]
    cols_mine_ref[...] = group_ref[core].astype(BF16)
    cols_other_ref[...] = group_ref[1 - core].astype(BF16)
    deep_mine_ref[...] = deep_ref[core].T.astype(BF16)
    deep_other_ref[...] = deep_ref[1 - core].T.astype(BF16)


def half_kernel(deep_ref, weight_ref, out_ref):
    out_ref[...] = nn(deep_ref[...], weight_ref[...])


def unit_kernel(half_ref, deep_ref, weight_ref, unit_ref, norm_ref):
    proj = half_ref[...] + nn(deep_ref[...], weight_ref[...])
    norm = jnp.sqrt(jnp.sum(proj * proj, axis=1, keepdims=True) + EPS)
    unit_ref[...] = (proj / norm).astype(BF16)
    norm_ref[...] = norm


def main_kernel(scal_ref, spot_ref, unit_ref, norm_ref, text_ref, back_ref, part_hbm,
                grad_ref, part_ref, sem):
    temper, offset, factor = scal_ref[0], scal_ref[1], scal_ref[2]
    unit = unit_ref[...]
    rows = unit.shape[0]
    pair = rows // 2
    row_id = lax.broadcasted_iota(jnp.int32, (rows, CHUNK), 0) - spot_ref[0]
    col_id = lax.broadcasted_iota(jnp.int32, (rows, CHUNK), 1) - spot_ref[1]
    inside = (row_id >= 0) & (row_id < pair)
    stores = []
    for k in range(text_ref.shape[0] // CHUNK):
        block = pl.ds(k * CHUNK, CHUNK)
        logits = temper * nt(unit, text_ref[block, :]) + offset
        same = inside & (col_id + k * CHUNK == row_id)
        weight = jnp.where(same, -factor, factor)
        grad = (weight / (1.0 + jnp.exp(jnp.where(same, logits, -logits)))).astype(BF16)
        grad_ref[:, block] = grad
        part_ref[block, :] = tn(grad, unit).astype(BF16)
        store = pltpu.make_async_copy(part_ref.at[block], part_hbm.at[block], sem.at[k])
        store.start()
        stores.append(store)
    image_back = nn(grad_ref[...], text_ref[...])
    unit_float = unit.astype(F32)
    radial = jnp.sum(unit_float * image_back, axis=1, keepdims=True)
    back = ((image_back - unit_float * radial) * (temper / norm_ref[...])).astype(BF16)
    back_ref[...] = back
    for store in stores:
        store.wait()


def join_kernel(own_ref, cols_ref, back_ref, out_ref):
    out_ref[...] = (own_ref[...] + nn(cols_ref[...], back_ref[...])).astype(BF16)


def fold_kernel(came_ref, out_ref, sum_ref, flat_ref):
    share = sum_ref.shape[0]
    total = None
    for k in range(came_ref.shape[0]):
        both = came_ref[k].astype(F32)
        both = both[:share] + both[share:]
        total = both if total is None else total + both
    sum_ref[...] = total
    flat_ref[...] = jnp.zeros_like(flat_ref)
    pieces = flat_ref.shape[0]
    size = sum_ref.shape[0] // pieces
    for p in range(pieces):
        for t in range(sum_ref.shape[1] // LANES):
            flat_ref[p, t * size:(t + 1) * size, :] = sum_ref[p * size:(p + 1) * size, t * LANES:(t + 1) * LANES]
    out_ref[...] = flat_ref[...].astype(BF16)


def unfold_kernel(came_ref, out_ref, sum_ref):
    total = came_ref[0].astype(F32)
    for k in range(1, came_ref.shape[0]):
        total += came_ref[k].astype(F32)
    sum_ref[...] = total
    size = out_ref.shape[0]
    for t in range(out_ref.shape[1] // LANES):
        out_ref[:, t * LANES:(t + 1) * LANES] = sum_ref[t * size:(t + 1) * size, :]


def place_kernel(scal_ref, chosen_ref, back_ref, unit_ref, norm_ref, out_ref):
    back = scal_ref[0] * back_ref[...].astype(F32)
    unit = unit_ref[...].astype(F32)
    radial = jnp.sum(unit * back, axis=1, keepdims=True)
    rest = (back - unit * radial) / norm_ref[...]
    spots = lax.broadcasted_iota(jnp.int32, (out_ref.shape[0], rest.shape[0]), 0)
    here = (spots == chosen_ref[...]).astype(BF16)
    placed = None
    for _ in range(3):
        part = rest.astype(BF16)
        rest = rest - part.astype(F32)
        placed = nn(here, part) if placed is None else placed + nn(here, part)
    out_ref[...] = placed


def call(kernel, outs, in_specs, out_specs, scratch=(), cost=0, limit=LIMIT):
    return pl.pallas_call(
        kernel,
        out_shape=tuple(jax.ShapeDtypeStruct(shape, dtype) for shape, dtype in outs),
        in_specs=in_specs,
        out_specs=out_specs,
        scratch_shapes=list(scratch),
        compiler_params=pltpu.CompilerParams(vmem_limit_bytes=limit),
        cost_estimate=pl.CostEstimate(flops=cost, bytes_accessed=2_000_000, transcendentals=0),
    )


def shards(image_cand, text_cand, selection, head_weight, logit_temp, logit_offset, loss_scale):
    pairs = selection.shape[0]
    cands, depth = image_cand.shape
    own_rows, width = head_weight.shape
    rows = 2 * pairs
    n_y, n_x, n_zh = lax.axis_size("y"), lax.axis_size("x"), lax.axis_size("zh")
    my_zl, my_y, core = (lax.axis_index(a) for a in ("zl", "y", "c"))
    total = pairs * lax.axis_size(ALL)
    spot = jnp.stack([my_zl * pairs, my_y * pairs, core])
    scalars = jnp.stack([logit_temp[0], logit_offset[0], loss_scale[0] / total])

    chosen = selection[None, :]
    text_unit, txt_norm = call(
        text_kernel, [((pairs, width), BF16), ((pairs, 1), F32)], [HBM] * 2, (VMEM,) * 2,
        [pltpu.VMEM((1, pairs), jnp.int32), pltpu.VMEM((cands, depth), BF16), pltpu.SemaphoreType.DMA((2,))],
        cost=2 * pairs * cands * width, limit=WHOLE,
    )(chosen, text_cand)
    text_all = lax.all_gather(text_unit, "y", axis=0, tiled=True)

    part = jnp.pad(head_weight, ((0, PADDED - own_rows), (0, 0)))
    slab = lax.all_gather(part, "zh", axis=0, tiled=True)
    slab, chosen = lax.optimization_barrier((slab, chosen))
    (picked,) = call(
        image_kernel, [((pairs, depth), BF16)], [VMEM, VMEM], (VMEM,), cost=2 * pairs * cands * depth,
    )(chosen, image_cand)
    there = hop(picked, "zl", 1)
    slabs = lax.all_to_all(jnp.broadcast_to(slab[None], (n_x,) + slab.shape), "x", 0, 0)
    mine = slabs.reshape(n_x * slab.shape[0], width)
    deep = mine.shape[0]
    deep_mine, deep_other, cols_mine, cols_other = call(
        lambda *refs: pair_kernel(own_rows, n_zh, *refs),
        [((rows, deep), BF16), ((rows, deep), BF16), ((depth // 2, rows), BF16), ((depth // 2, rows), BF16)],
        [SMEM, VMEM, VMEM], (VMEM,) * 4,
        [pltpu.VMEM((depth, rows), F32), pltpu.VMEM((2, depth // 2, rows), F32), pltpu.VMEM((2, deep, rows), F32)],
    )(spot, picked, there)
    cols_there = hop(cols_other, "c", 1)
    mine, cols_there = lax.optimization_barrier((mine, cols_there))
    other = hop(mine, "c", 1)
    (half,) = call(
        half_kernel, [((rows, width), F32)], [VMEM, VMEM], (VMEM,), cost=2 * rows * deep * width, limit=4 * 1024 * 1024,
    )(deep_mine, mine)
    image_unit, img_norm = call(
        unit_kernel, [((rows, width), BF16), ((rows, 1), F32)], [VMEM] * 3, (VMEM,) * 2, cost=2 * rows * deep * width,
    )(half, deep_other, other)
    proj_back, text_part = call(
        main_kernel,
        [((rows, width), BF16), ((n_y * pairs, width), BF16)],
        [SMEM, SMEM] + [VMEM] * 3, (VMEM, HBM),
        [pltpu.VMEM((rows, n_y * pairs), BF16), pltpu.VMEM((n_y * pairs, width), BF16),
         pltpu.SemaphoreType.DMA((n_y * pairs // CHUNK,))],
        cost=6 * rows * n_y * pairs * width, limit=ROOMY,
    )(scalars, spot, image_unit, img_norm, text_all)
    text_back = lax.psum_scatter(text_part.reshape(n_y, pairs, width), "y", scatter_dimension=0)
    back_there = hop(proj_back, "c", 1)
    (own,) = call(
        half_kernel, [((depth // 2, width), F32)], [VMEM] * 2, (VMEM,), cost=rows * depth * width,
    )(cols_mine, proj_back)
    (head,) = call(
        join_kernel, [((depth // 2, width), BF16)], [VMEM] * 3, (VMEM,), cost=rows * depth * width,
    )(own, cols_there, back_there)

    share = depth // 4 // n_x
    came = lax.all_to_all(head.reshape(2 * n_x, share, width), ("x", "zl"), 0, 0)
    piece = share // n_zh
    strips = piece * (width // LANES)
    strips += -strips % 16
    (folded,) = call(
        fold_kernel, [((n_zh, strips, LANES), BF16)], [VMEM], (VMEM,),
        [pltpu.VMEM((share, width), F32), pltpu.VMEM((n_zh, strips, LANES), F32)],
    )(came.reshape(n_x, 2 * share, width))
    came = lax.all_to_all(folded, "zh", 0, 0)
    head = jnp.sum(came.astype(F32), axis=0).astype(BF16)
    came = lax.all_to_all(jnp.broadcast_to(head[None], (n_y,) + head.shape), "y", 0, 0)
    (head,) = call(unfold_kernel, [((piece, width), F32)], [VMEM], (VMEM,), [pltpu.VMEM((strips, LANES), F32)])(came)

    there = hop(head, "zl", 1)
    (text_grad,) = call(
        place_kernel, [((cands, width), F32)], [SMEM] + [VMEM] * 4, (VMEM,), cost=6 * cands * pairs * width,
    )(scalars, chosen, text_back, text_unit, txt_norm)
    there, text_grad = lax.optimization_barrier((there, text_grad))
    head_grad = jnp.concatenate([jnp.where(my_zl == 0, head, there), jnp.where(my_zl == 0, there, head)], axis=0)
    return head_grad, text_grad


def solution(mesh):
    devices = mesh.devices
    fine = Mesh(devices.reshape(2, devices.shape[0] // 2, 4, devices.shape[1] // 8, 2), ALL)
    return jax.shard_map(
        shards,
        mesh=fine,
        in_specs=(P(ALL, None), P(ALL, None), P(ALL), P(("x", "zh", "c"), None), P(), P(), P()),
        out_specs=(P(("x", "zh", "c"), None), P(ALL, None)),
        check_vma=False,
    )
```

```python
import jax
import jax.numpy as jnp
from jax import lax
from jax.experimental import pallas as pl
from jax.experimental.pallas import tpu as pltpu
from jax.sharding import Mesh, PartitionSpec as P

EPS = 1e-06
ALL = ("zl", "y", "x", "zh", "c")
PADDED = 40
CHUNK = 512
VMEM = pl.BlockSpec(memory_space=pltpu.VMEM)
SMEM = pl.BlockSpec(memory_space=pltpu.SMEM)
HBM = pl.BlockSpec(memory_space=pltpu.HBM)
LANES = 128
LIMIT = 8 * 1024 * 1024
ROOMY = 12 * 1024 * 1024
WHOLE = 61 * 1024 * 1024
F32, BF16 = jnp.float32, jnp.bfloat16


def hop(value, axis, steps):
    count = lax.axis_size(axis)
    return lax.ppermute(value, axis, [(s, (s + steps) % count) for s in range(count)])


def nn(a, b):
    return jnp.dot(a, b, preferred_element_type=F32)


def nt(a, b):
    return lax.dot_general(a, b, (((1,), (1,)), ((), ())), preferred_element_type=F32)


def tn(a, b):
    return lax.dot_general(a, b, (((0,), (0,)), ((), ())), preferred_element_type=F32)


def pick_rows(chosen, cands):
    spots = lax.broadcasted_iota(jnp.int32, (cands.shape[0], chosen.shape[1]), 0)
    return tn((spots == chosen).astype(BF16), cands)


def text_kernel(chosen_hbm, cand_hbm, unit_ref, norm_ref, chosen_ref, cand_ref, sem):
    loads = [pltpu.make_async_copy(source, target, sem.at[k]) for k, (source, target) in enumerate(
        ((chosen_hbm, chosen_ref), (cand_hbm, cand_ref)))]
    for load in loads:
        load.start()
    for load in loads:
        load.wait()
    texts = pick_rows(chosen_ref[...], cand_ref[...])
    norm = jnp.sqrt(jnp.sum(texts * texts, axis=1, keepdims=True) + EPS)
    unit_ref[...] = (texts / norm).astype(BF16)
    norm_ref[...] = norm


def image_kernel(chosen_ref, cand_ref, out_ref):
    out_ref[...] = pick_rows(chosen_ref[...], cand_ref[...]).astype(BF16)


def pair_kernel(size, n_zh, spot_ref, mine_ref, there_ref, deep_mine_ref, deep_other_ref, cols_mine_ref, cols_other_ref,
                flat_ref, group_ref, deep_ref):
    pairs, depth = mine_ref.shape
    first = spot_ref[0] == 0
    mine, there = mine_ref[...].astype(F32).T, there_ref[...].astype(F32).T
    flat_ref[:, :pairs] = jnp.where(first, mine, there)
    flat_ref[:, pairs:] = jnp.where(first, there, mine)
    deep_ref[...] = jnp.zeros_like(deep_ref)
    for block in range(depth // size):
        core, place = block % 2, block // 2
        rows = flat_ref[block * size:(block + 1) * size, :]
        part = size // 2
        start = (place // n_zh * 2 * n_zh + place % n_zh) * part
        group_ref[core, start:start + part, :] = rows[:part]
        group_ref[core, start + n_zh * part:start + (n_zh + 1) * part, :] = rows[part:]
        deep_ref[core, place * PADDED:place * PADDED + size, :] = rows
    core = spot_ref[2]
    cols_mine_ref[...] = group_ref[core].astype(BF16)
    cols_other_ref[...] = group_ref[1 - core].astype(BF16)
    deep_mine_ref[...] = deep_ref[core].T.astype(BF16)
    deep_other_ref[...] = deep_ref[1 - core].T.astype(BF16)


def half_kernel(deep_ref, weight_ref, out_ref):
    out_ref[...] = nn(deep_ref[...], weight_ref[...])


def unit_kernel(half_ref, deep_ref, weight_ref, unit_ref, norm_ref):
    proj = half_ref[...] + nn(deep_ref[...], weight_ref[...])
    norm = jnp.sqrt(jnp.sum(proj * proj, axis=1, keepdims=True) + EPS)
    unit_ref[...] = (proj / norm).astype(BF16)
    norm_ref[...] = norm


def main_kernel(scal_ref, spot_ref, unit_ref, norm_ref, text_ref, back_ref, part_hbm,
                grad_ref, part_ref, sem):
    temper, offset, factor = scal_ref[0], scal_ref[1], scal_ref[2]
    unit = unit_ref[...]
    rows = unit.shape[0]
    pair = rows // 2
    row_id = lax.broadcasted_iota(jnp.int32, (rows, CHUNK), 0) - spot_ref[0]
    col_id = lax.broadcasted_iota(jnp.int32, (rows, CHUNK), 1) - spot_ref[1]
    inside = (row_id >= 0) & (row_id < pair)
    stores = []
    for k in range(text_ref.shape[0] // CHUNK):
        block = pl.ds(k * CHUNK, CHUNK)
        logits = temper * nt(unit, text_ref[block, :]) + offset
        same = inside & (col_id + k * CHUNK == row_id)
        weight = jnp.where(same, -factor, factor)
        grad = (weight / (1.0 + jnp.exp(jnp.where(same, logits, -logits)))).astype(BF16)
        grad_ref[:, block] = grad
        part_ref[block, :] = tn(grad, unit).astype(BF16)
        store = pltpu.make_async_copy(part_ref.at[block], part_hbm.at[block], sem.at[k])
        store.start()
        stores.append(store)
    image_back = nn(grad_ref[...], text_ref[...])
    unit_float = unit.astype(F32)
    radial = jnp.sum(unit_float * image_back, axis=1, keepdims=True)
    back = ((image_back - unit_float * radial) * (temper / norm_ref[...])).astype(BF16)
    back_ref[...] = back
    for store in stores:
        store.wait()


def join_kernel(own_ref, cols_ref, back_ref, out_ref):
    out_ref[...] = (own_ref[...] + nn(cols_ref[...], back_ref[...])).astype(BF16)


def fold_kernel(came_ref, out_ref, sum_ref, flat_ref):
    share = sum_ref.shape[0]
    total = None
    for k in range(came_ref.shape[0]):
        both = came_ref[k].astype(F32)
        both = both[:share] + both[share:]
        total = both if total is None else total + both
    sum_ref[...] = total
    flat_ref[...] = jnp.zeros_like(flat_ref)
    pieces = flat_ref.shape[0]
    size = sum_ref.shape[0] // pieces
    for p in range(pieces):
        for t in range(sum_ref.shape[1] // LANES):
            flat_ref[p, t * size:(t + 1) * size, :] = sum_ref[p * size:(p + 1) * size, t * LANES:(t + 1) * LANES]
    out_ref[...] = flat_ref[...].astype(BF16)


def unfold_kernel(spot_ref, mine_ref, there_ref, out_ref, pair_ref):
    first = spot_ref[0] == 0
    mine, there = mine_ref[...], there_ref[...]
    pair_ref[0] = jnp.where(first, mine, there)
    pair_ref[1] = jnp.where(first, there, mine)
    size = out_ref.shape[0] // 2
    for half in range(2):
        for t in range(out_ref.shape[1] // LANES):
            out_ref[half * size:(half + 1) * size, t * LANES:(t + 1) * LANES] = pair_ref[half, t * size:(t + 1) * size, :]


def place_kernel(scal_ref, chosen_ref, back_ref, unit_ref, norm_ref, out_ref):
    back = scal_ref[0] * back_ref[...].astype(F32)
    unit = unit_ref[...].astype(F32)
    radial = jnp.sum(unit * back, axis=1, keepdims=True)
    rest = (back - unit * radial) / norm_ref[...]
    spots = lax.broadcasted_iota(jnp.int32, (out_ref.shape[0], rest.shape[0]), 0)
    here = (spots == chosen_ref[...]).astype(BF16)
    placed = None
    for _ in range(3):
        part = rest.astype(BF16)
        rest = rest - part.astype(F32)
        placed = nn(here, part) if placed is None else placed + nn(here, part)
    out_ref[...] = placed


def call(kernel, outs, in_specs, out_specs, scratch=(), cost=0, limit=LIMIT):
    return pl.pallas_call(
        kernel,
        out_shape=tuple(jax.ShapeDtypeStruct(shape, dtype) for shape, dtype in outs),
        in_specs=in_specs,
        out_specs=out_specs,
        scratch_shapes=list(scratch),
        compiler_params=pltpu.CompilerParams(vmem_limit_bytes=limit),
        cost_estimate=pl.CostEstimate(flops=cost, bytes_accessed=2_000_000, transcendentals=0),
    )


def shards(image_cand, text_cand, selection, head_weight, logit_temp, logit_offset, loss_scale):
    pairs = selection.shape[0]
    cands, depth = image_cand.shape
    own_rows, width = head_weight.shape
    rows = 2 * pairs
    n_y, n_x, n_zh = lax.axis_size("y"), lax.axis_size("x"), lax.axis_size("zh")
    my_zl, my_y, core = (lax.axis_index(a) for a in ("zl", "y", "c"))
    total = pairs * lax.axis_size(ALL)
    spot = jnp.stack([my_zl * pairs, my_y * pairs, core])
    scalars = jnp.stack([logit_temp[0], logit_offset[0], loss_scale[0] / total])

    chosen = selection[None, :]
    text_unit, txt_norm = call(
        text_kernel, [((pairs, width), BF16), ((pairs, 1), F32)], [HBM] * 2, (VMEM,) * 2,
        [pltpu.VMEM((1, pairs), jnp.int32), pltpu.VMEM((cands, depth), BF16), pltpu.SemaphoreType.DMA((2,))],
        cost=2 * pairs * cands * width, limit=WHOLE,
    )(chosen, text_cand)
    text_all = lax.all_gather(text_unit, "y", axis=0, tiled=True)

    part = jnp.pad(head_weight, ((0, PADDED - own_rows), (0, 0)))
    slab = lax.all_gather(part, "zh", axis=0, tiled=True)
    slab, chosen = lax.optimization_barrier((slab, chosen))
    (picked,) = call(
        image_kernel, [((pairs, depth), BF16)], [VMEM, VMEM], (VMEM,), cost=2 * pairs * cands * depth,
    )(chosen, image_cand)
    there = hop(picked, "zl", 1)
    slabs = lax.all_to_all(jnp.broadcast_to(slab[None], (n_x,) + slab.shape), "x", 0, 0)
    mine = slabs.reshape(n_x * slab.shape[0], width)
    deep = mine.shape[0]
    deep_mine, deep_other, cols_mine, cols_other = call(
        lambda *refs: pair_kernel(own_rows, n_zh, *refs),
        [((rows, deep), BF16), ((rows, deep), BF16), ((depth // 2, rows), BF16), ((depth // 2, rows), BF16)],
        [SMEM, VMEM, VMEM], (VMEM,) * 4,
        [pltpu.VMEM((depth, rows), F32), pltpu.VMEM((2, depth // 2, rows), F32), pltpu.VMEM((2, deep, rows), F32)],
    )(spot, picked, there)
    cols_there = hop(cols_other, "c", 1)
    mine, cols_there = lax.optimization_barrier((mine, cols_there))
    other = hop(mine, "c", 1)
    (half,) = call(
        half_kernel, [((rows, width), F32)], [VMEM, VMEM], (VMEM,), cost=2 * rows * deep * width, limit=4 * 1024 * 1024,
    )(deep_mine, mine)
    image_unit, img_norm = call(
        unit_kernel, [((rows, width), BF16), ((rows, 1), F32)], [VMEM] * 3, (VMEM,) * 2, cost=2 * rows * deep * width,
    )(half, deep_other, other)
    proj_back, text_part = call(
        main_kernel,
        [((rows, width), BF16), ((n_y * pairs, width), BF16)],
        [SMEM, SMEM] + [VMEM] * 3, (VMEM, HBM),
        [pltpu.VMEM((rows, n_y * pairs), BF16), pltpu.VMEM((n_y * pairs, width), BF16),
         pltpu.SemaphoreType.DMA((n_y * pairs // CHUNK,))],
        cost=6 * rows * n_y * pairs * width, limit=ROOMY,
    )(scalars, spot, image_unit, img_norm, text_all)
    text_back = lax.psum_scatter(text_part.reshape(n_y, pairs, width), "y", scatter_dimension=0)
    back_there = hop(proj_back, "c", 1)
    (own,) = call(
        half_kernel, [((depth // 2, width), F32)], [VMEM] * 2, (VMEM,), cost=rows * depth * width,
    )(cols_mine, proj_back)
    (head,) = call(
        join_kernel, [((depth // 2, width), BF16)], [VMEM] * 3, (VMEM,), cost=rows * depth * width,
    )(own, cols_there, back_there)

    share = depth // 4 // n_x
    came = lax.all_to_all(head.reshape(2 * n_x, share, width), ("x", "zl"), 0, 0)
    piece = share // n_zh
    strips = piece * (width // LANES)
    strips += -strips % 16
    (folded,) = call(
        fold_kernel, [((n_zh, strips, LANES), BF16)], [VMEM], (VMEM,),
        [pltpu.VMEM((share, width), F32), pltpu.VMEM((n_zh, strips, LANES), F32)],
    )(came.reshape(n_x, 2 * share, width))
    came = lax.all_to_all(folded, "zh", 0, 0)
    head = jnp.sum(came.astype(F32), axis=0).astype(BF16)
    came = lax.all_to_all(jnp.broadcast_to(head[None], (n_y,) + head.shape), "y", 0, 0)
    head = jnp.sum(came.astype(F32), axis=0)
    there = hop(head, "zl", 1)
    (text_grad,) = call(
        place_kernel, [((cands, width), F32)], [SMEM] + [VMEM] * 4, (VMEM,), cost=6 * cands * pairs * width,
    )(scalars, chosen, text_back, text_unit, txt_norm)
    there, text_grad = lax.optimization_barrier((there, text_grad))
    (head_grad,) = call(
        unfold_kernel, [((own_rows, width), F32)], [SMEM, VMEM, VMEM], (VMEM,), [pltpu.VMEM((2, strips, LANES), F32)],
    )(spot, head, there)
    return head_grad, text_grad


def solution(mesh):
    devices = mesh.devices
    fine = Mesh(devices.reshape(2, devices.shape[0] // 2, 4, devices.shape[1] // 8, 2), ALL)
    return jax.shard_map(
        shards,
        mesh=fine,
        in_specs=(P(ALL, None), P(ALL, None), P(ALL), P(("x", "zh", "c"), None), P(), P(), P()),
        out_specs=(P(("x", "zh", "c"), None), P(ALL, None)),
        check_vma=False,
    )
```
